32 devices in a mesh: groups: 2 (over y), train: 4 (over z), query: 2 (over x), feat: 2 (over core).
Axes of the slice: x: 2, y: 2, z: 4, core: 2. Of those that a mesh axis runs over, the one named last changes fastest.
Arguments:
- train_pool: float32 [320, 8192], P(('groups', 'train'), 'feat'), parts along dimension 0, may hold values from -130 to 130
- query_pool: float32 [864, 8192], P(('groups', 'query'), 'feat'), parts along dimension 0, may hold values from -16640 to 16640
- train_pick: int32 [256], P(('groups', 'train')), parts along dimension 0, may hold values from 0 to 159, as said below
- query_pick: int32 [768], P(('groups', 'query')), parts along dimension 0, may hold values from 0 to 431, as said below
Outputs:
- scores: float32 [768, 128], P(('groups', 'query'), 'train'), parts along dimension 0
The draws below stay inside these ranges and needn't reach their ends.
There are 2 independent parts, one for each index of `groups`. The reference program is written for one: setup_inputs(seed, part) draws one part's arguments, and reference() takes and returns one part's arrays. A program takes and returns all parts, laid end to end along the dimension named above; each array names one. Nothing has to cross between parts.
Inputs may be any that keep to these rules, and one draw needn't show every extreme that they name: `train_pick`: the entries for training block t (positions t * 32 to (t + 1) * 32 - 1) are distinct and lie in t * 40 to (t + 1) * 40 - 1. `query_pick`: the entries for query block q (positions q * 192 to (q + 1) * 192 - 1) are distinct and lie in q * 216 to (q + 1) * 216 - 1.
All inputs are finite; a program needn't handle non-finite values.
Results may differ from the reference program's by a relative error of at most 0.0003.
Values sent between devices are 32-bit elements; how exact they have to be, the bound alone decides.
A program may use at most 64 MiB of HBM per device.

```python
import math
import jax
import jax.numpy as jnp
from jax import lax

WIDTH = 8192
TRAIN_DEV = 32
QUERY_DEV = 192
TRAIN_POOL = 40
QUERY_POOL = 216
N_TRAIN = 4
N_QUERY = 2


def shared_directions(key):
    return jnp.clip(jax.random.normal(jax.random.fold_in(key, 91), (3, WIDTH), jnp.float32), -4.0, 4.0)


def mixture(noise, coeffs, scales, directions):
    mixed = noise + coeffs[:, 0:1] * directions[0][None, :]
    mixed = mixed + coeffs[:, 1:2] * directions[1][None, :]
    mixed = mixed + coeffs[:, 2:3] * directions[2][None, :]
    return scales[:, None] * mixed


def draw_train_pool(key, part):
    directions = shared_directions(key)
    key = jax.random.fold_in(key, 3)
    key_noise, key_coeff, key_scale = jax.random.split(key, 3)
    count = TRAIN_POOL * N_TRAIN
    coeffs = jnp.clip(jax.random.normal(key_coeff, (count, 3), jnp.float32), -3.0, 3.0)
    noise = jnp.clip(jax.random.normal(key_noise, (count, WIDTH), jnp.float32), -6.0, 6.0)
    scales = jnp.exp(jax.random.uniform(key_scale, (count,), jnp.float32, math.log(0.5), math.log(2.0)))
    return mixture(noise, coeffs, scales, directions)


def draw_query_pool(key, part):
    directions = shared_directions(key)
    key = jax.random.fold_in(key, 5)
    key_noise, key_coeff, key_scale = jax.random.split(key, 3)
    count = QUERY_POOL * N_QUERY
    coeffs = jnp.clip(jax.random.normal(key_coeff, (count, 3), jnp.float32), -3.0, 3.0)
    noise = jnp.clip(jax.random.normal(key_noise, (count, WIDTH), jnp.float32), -6.0, 6.0)
    scales = jnp.exp(jax.random.uniform(key_scale, (count,), jnp.float32, math.log(0.5), math.log(2.0)))
    return 128.0 * mixture(noise, coeffs, scales, directions)


def block_picks(key, blocks, pool_rows, taken):
    keys = jax.random.split(key, blocks)
    orders = jax.vmap(lambda single: jax.random.permutation(single, pool_rows))(keys)
    offsets = jnp.arange(blocks, dtype=jnp.int32)[:, None] * pool_rows
    return (orders[:, :taken].astype(jnp.int32) + offsets).reshape(-1)


def draw_train_pick(key, part):
    key = jax.random.fold_in(key, 7)
    return block_picks(key, N_TRAIN, TRAIN_POOL, TRAIN_DEV)


def draw_query_pick(key, part):
    key = jax.random.fold_in(key, 11)
    return block_picks(key, N_QUERY, QUERY_POOL, QUERY_DEV)


def setup_inputs(seed: int = 0, part: int = 0) -> dict:
    key_of = jax.random.split(jax.random.key(seed), 5)
    part_splits = jax.random.split(jax.random.fold_in(key_of[4], part), 5)
    return {
        "train_pool": draw_train_pool(jax.random.fold_in(jax.random.fold_in(key_of[4], part), 71), part),
        "query_pool": draw_query_pool(jax.random.fold_in(jax.random.fold_in(key_of[4], part), 71), part),
        "train_pick": draw_train_pick(jax.random.fold_in(jax.random.fold_in(key_of[4], part), 71), part),
        "query_pick": draw_query_pick(jax.random.fold_in(jax.random.fold_in(key_of[4], part), 71), part),
    }


def reference(train_pool, query_pool, train_pick, query_pick):
    highest = lax.Precision.HIGHEST
    train_rows = jnp.take(train_pool, train_pick, axis=0)
    query_rows = jnp.take(query_pool, query_pick, axis=0)
    kernel = jnp.dot(train_rows.astype(jnp.float32), train_rows.T.astype(jnp.float32), precision=highest, preferred_element_type=jnp.float32)
    cross_tile = jnp.dot(query_rows.astype(jnp.float32), train_rows.T.astype(jnp.float32), precision=highest, preferred_element_type=jnp.float32)
    identity = jnp.eye(kernel.shape[0], dtype=jnp.float32)
    factor = jnp.linalg.cholesky(kernel + 0.5 * WIDTH * identity)
    halfway = lax.linalg.triangular_solve(factor, cross_tile.T, left_side=True, lower=True)
    solved = lax.linalg.triangular_solve(factor, halfway, left_side=True, lower=True, transpose_a=True)
    return solved.T
```

```python
import functools

import jax
import jax.numpy as jnp
from jax import lax
from jax.experimental import pallas as pl
from jax.experimental.pallas import tpu as pltpu
from jax.sharding import PartitionSpec as P

WIDTH = 8192
HIGHEST = lax.Precision.HIGHEST
NT = (((1,), (1,)), ((), ()))
CHUNKS = 4


def dot_nt(a, b):
    return lax.dot_general(a, b, NT, precision=HIGHEST, preferred_element_type=jnp.float32)


def products(n_train, n_query, n_feat, train_pick, query_pick, train_pool, query_pool,
             kernel_out, cross_out,
             train_buf, query_buf, rows, blocks, part, terms, slab, full, mine, other, tile, crosses,
             local_sem, a2a_send, a2a_recv, rs_send, rs_recv, ag_send, ag_recv,
             pair_send, pair_recv, tile_send, tile_recv):
    g = lax.axis_index("groups")
    t = lax.axis_index("train")
    q = lax.axis_index("query")
    f = lax.axis_index("feat")
    n_pool, width = train_pool.shape
    block_rows = train_pick.shape[0]
    step = width // CHUNKS
    load_train = pltpu.make_async_copy(train_pool, train_buf, local_sem.at[CHUNKS])
    load_train.start()
    loads = []
    for c in range(CHUNKS):
        cols = pl.ds(c * step, step)
        load = pltpu.make_async_copy(query_pool.at[:, cols], query_buf.at[:, cols], local_sem.at[c])
        load.start()
        loads.append(load)

    offsets = [
        (a, b, c) for a in range(n_train) for b in range(n_query) for c in range(n_feat)
    ][1:]

    def peer(a, b, c):
        return lax.rem(t + a, n_train), lax.rem(q + b, n_query), lax.rem(f + c, n_feat)

    def device(where):
        return (g, where[0], where[1], where[2])

    def place(where):
        return (where[0] * n_query + where[1]) * n_feat + where[2]

    barrier = pltpu.get_barrier_semaphore()
    for off in offsets:
        pl.semaphore_signal(
            barrier, inc=1, device_id=device(peer(*off)), device_id_type=pl.DeviceIdType.MESH
        )

    load_train.wait()
    for r in range(block_rows):
        named = jnp.clip(train_pick[r] - t * n_pool, 0, n_pool - 1)
        rows[r : r + 1, :] = train_buf[pl.ds(named, 1), :]
    pl.semaphore_wait(barrier, len(offsets))

    def remote(src, dst, send, recv, where):
        copy = pltpu.make_async_remote_copy(
            src_ref=src, dst_ref=dst, send_sem=send, recv_sem=recv,
            device_id=device(where), device_id_type=pl.DeviceIdType.MESH,
        )
        copy.start()
        return copy

    share = width // (n_train * n_query)
    a2a = []
    for a in range(1, n_train):
        where = peer(a, 0, 0)
        cols = pl.ds(pl.multiple_of((where[0] * n_query + q) * share, share), share)
        a2a.append(remote(rows.at[:, cols], blocks.at[t], a2a_send.at[a], a2a_recv.at[a], where))
    cols = pl.ds(pl.multiple_of((t * n_query + q) * share, share), share)
    blocks[t] = rows[:, cols]

    total = None
    for c in range(CHUNKS):
        loads[c].wait()
        term = dot_nt(rows[:, c * step : (c + 1) * step], query_buf[:, c * step : (c + 1) * step])
        total = term if total is None else total + term
    n_query_pool = query_pool.shape[0]
    n_queries = query_pick.shape[1]
    chosen = (
        lax.broadcasted_iota(jnp.int32, (n_query_pool, n_queries), 0)
        == query_pick[...] - q * n_query_pool
    ).astype(jnp.float32)
    mine[...] = jnp.dot(total, chosen, precision=HIGHEST, preferred_element_type=jnp.float32)
    pair = remote(mine, other, pair_send, pair_recv, peer(0, 0, 1))

    for copy in a2a:
        copy.wait()
    gathered = blocks[...].reshape(n_train * block_rows, share)
    part[...] = dot_nt(gathered, gathered)
    slab_rows = slab.shape[0]

    def slab_of(where):
        return pl.ds(pl.multiple_of(place(where) * slab_rows, slab_rows), slab_rows)

    here = (t, q, f)
    rs = []
    for i, off in enumerate(offsets):
        where = peer(*off)
        rs.append(remote(part.at[slab_of(where)], terms.at[i], rs_send.at[i], rs_recv.at[i], where))

    pair.wait()
    tile[...] = mine[...] + other[...]
    crosses[t] = tile[...]
    tiles = []
    for a in range(1, n_train):
        tiles.append(remote(tile, crosses.at[t], tile_send.at[a], tile_recv.at[a], peer(a, 0, 0)))

    for copy in rs:
        copy.wait()
    summed = part[slab_of(here), :]
    for i in range(len(offsets)):
        summed = summed + terms[i]
    slab[...] = summed
    full[slab_of(here), :] = summed
    ag = []
    for i, off in enumerate(offsets):
        ag.append(remote(slab, full.at[slab_of(here)], ag_send.at[i], ag_recv.at[i], peer(*off)))
    for copy in tiles:
        copy.wait()
    cross_out[...] = crosses[...].reshape(cross_out.shape)
    for copy in ag:
        copy.wait()
    kernel_out[...] = full[...]


def solve(kernel_ref, cross_ref, scores_ref, inverse):
    order = kernel_ref.shape[0]
    lane = lax.broadcasted_iota(jnp.int32, (8, order), 1)
    sub = lax.broadcasted_iota(jnp.int32, (8, order), 0)
    tiles = []
    for i in range(order // 8):
        diagonal = lane == sub + 8 * i
        tiles.append(kernel_ref[8 * i : 8 * i + 8, :] + jnp.where(diagonal, 0.5 * WIDTH, 0.0))
    for k in range(0, order, 2):
        home, r = k // 8, k % 8
        first = jnp.broadcast_to(tiles[home][r : r + 1, :], (8, order))
        second = jnp.broadcast_to(tiles[home][r + 1 : r + 2, :], (8, order))
        a = jnp.broadcast_to(first[:, k : k + 1], (8, order))
        b = jnp.broadcast_to(first[:, k + 1 : k + 2], (8, order))
        d = jnp.broadcast_to(second[:, k + 1 : k + 2], (8, order))
        inv_a = 1.0 / a
        ratio = b * inv_a
        inv_s = 1.0 / (d - b * ratio)
        at_k = lane == k
        at_k1 = lane == k + 1
        in_pair = at_k | at_k1
        first = jnp.where(in_pair, jnp.where(at_k, 1.0, 0.0), first)
        second = jnp.where(in_pair, jnp.where(at_k1, 1.0, 0.0), second)
        low = inv_s * (second - ratio * first)
        high = inv_a * first - ratio * low
        for i in range(order // 8):
            old = tiles[i]
            c0 = jnp.broadcast_to(old[:, k : k + 1], (8, order))
            c1 = jnp.broadcast_to(old[:, k + 1 : k + 2], (8, order))
            new = jnp.where(in_pair, 0.0, old) - c0 * high - c1 * low
            if i == home:
                new = jnp.where(sub == r, high, jnp.where(sub == r + 1, low, new))
            tiles[i] = new
    for i in range(order // 8):
        inverse[8 * i : 8 * i + 8, :] = tiles[i]
    columns = scores_ref.shape[1]
    start = pl.multiple_of(lax.axis_index("train") * columns, columns)
    scores_ref[...] = dot_nt(cross_ref[...].T, inverse[pl.ds(start, columns), :])


def with_kernels(sizes, train_pool, query_pool, train_pick, query_pick):
    n_train, n_query, n_feat = sizes
    n_peers = n_train * n_query * n_feat
    block_rows = train_pick.shape[0]
    order = block_rows * n_train
    n_queries = query_pick.shape[0]
    width = train_pool.shape[1]
    share = width // (n_train * n_query)
    slab_rows = order // n_peers
    vmem = pl.BlockSpec(memory_space=pltpu.VMEM)
    smem = pl.BlockSpec(memory_space=pltpu.SMEM)
    anywhere = pl.BlockSpec(memory_space=pl.ANY)
    f32 = jnp.float32
    dma = pltpu.SemaphoreType.DMA
    kernel, cross = pl.pallas_call(
        functools.partial(products, n_train, n_query, n_feat),
        out_shape=(
            jax.ShapeDtypeStruct((order, order), f32),
            jax.ShapeDtypeStruct((order, n_queries), f32),
        ),
        in_specs=[smem, vmem, anywhere, anywhere],
        out_specs=(vmem, vmem),
        scratch_shapes=[
            pltpu.VMEM(train_pool.shape, f32),
            pltpu.VMEM(query_pool.shape, f32),
            pltpu.VMEM((block_rows, width), f32),
            pltpu.VMEM((n_train, block_rows, share), f32),
            pltpu.VMEM((order, order), f32),
            pltpu.VMEM((n_peers - 1, slab_rows, order), f32),
            pltpu.VMEM((slab_rows, order), f32),
            pltpu.VMEM((order, order), f32),
            pltpu.VMEM((block_rows, n_queries), f32),
            pltpu.VMEM((block_rows, n_queries), f32),
            pltpu.VMEM((block_rows, n_queries), f32),
            pltpu.VMEM((n_train, block_rows, n_queries), f32),
            dma((CHUNKS + 1,)),
            dma((n_train,)), dma((n_train,)),
            dma((n_peers - 1,)), dma((n_peers - 1,)),
            dma((n_peers - 1,)), dma((n_peers - 1,)),
            dma, dma,
            dma((n_train,)), dma((n_train,)),
        ],
        compiler_params=pltpu.CompilerParams(
            collective_id=0, has_side_effects=True, vmem_limit_bytes=32 * 1024 * 1024
        ),
        name="products",
    )(train_pick, query_pick.reshape(1, n_queries), train_pool, query_pool)
    return pl.pallas_call(
        solve,
        out_shape=jax.ShapeDtypeStruct((n_queries, block_rows), f32),
        in_specs=[vmem, vmem],
        out_specs=vmem,
        scratch_shapes=[pltpu.VMEM((order, order), f32)],
        compiler_params=pltpu.CompilerParams(vmem_limit_bytes=32 * 1024 * 1024),
        name="solve",
    )(kernel, cross)


def with_arrays(train_pool, query_pool, train_pick, query_pick):
    block_rows = train_pick.shape[0]
    train_index = lax.axis_index("train")
    query_index = lax.axis_index("query")
    train_rows = jnp.take(train_pool, train_pick - train_index * train_pool.shape[0], axis=0)
    query_rows = jnp.take(query_pool, query_pick - query_index * query_pool.shape[0], axis=0)
    cross_tile = dot_nt(query_rows, train_rows)
    kernel_part = dot_nt(train_rows, lax.all_gather(train_rows, "train", axis=0, tiled=True))
    cross_tile, kernel_part = lax.psum((cross_tile, kernel_part), "feat")
    kernel = lax.all_gather(kernel_part, "train", axis=0, tiled=True)
    order = kernel.shape[0]
    factor = jnp.linalg.cholesky(kernel + 0.5 * WIDTH * jnp.eye(order, dtype=jnp.float32))
    sel_rows = lax.broadcasted_iota(jnp.int32, (order, block_rows), 0)
    sel_cols = lax.broadcasted_iota(jnp.int32, (order, block_rows), 1) + train_index * block_rows
    selector = (sel_rows == sel_cols).astype(jnp.float32)
    halfway = lax.linalg.triangular_solve(factor, selector, left_side=True, lower=True)
    inverse_cols = lax.linalg.triangular_solve(
        factor, halfway, left_side=True, lower=True, transpose_a=True
    )
    return jnp.dot(
        lax.all_gather(cross_tile, "train", axis=1, tiled=True),
        inverse_cols,
        precision=HIGHEST,
        preferred_element_type=jnp.float32,
    )


def solution(mesh):
    sizes = mesh.shape["train"], mesh.shape["query"], mesh.shape["feat"]

    def on_device(train_pool, query_pool, train_pick, query_pick):
        order = train_pick.shape[0] * sizes[0]
        fits = (
            order == 128
            and order % (8 * sizes[0] * sizes[1] * sizes[2]) == 0
            and train_pool.shape[1] % (128 * sizes[0] * sizes[1]) == 0
        )
        if fits:
            return with_kernels(sizes, train_pool, query_pool, train_pick, query_pick)
        return with_arrays(train_pool, query_pool, train_pick, query_pick)

    return jax.shard_map(
        on_device,
        mesh=mesh,
        in_specs=(
            P(("groups", "train"), "feat"),
            P(("groups", "query"), "feat"),
            P(("groups", "train")),
            P(("groups", "query")),
        ),
        out_specs=P(("groups", "query"), "train"),
        check_vma=False,
    )
```

```python
import functools

import jax
import jax.numpy as jnp
from jax import lax
from jax.experimental import pallas as pl
from jax.experimental.pallas import tpu as pltpu
from jax.sharding import PartitionSpec as P

WIDTH = 8192
HIGHEST = lax.Precision.HIGHEST
NT = (((1,), (1,)), ((), ()))
CHUNKS = 4


def dot_nt(a, b):
    return lax.dot_general(a, b, NT, precision=HIGHEST, preferred_element_type=jnp.float32)


def products(n_train, n_query, n_feat, train_pick_in, query_pick_in, train_pool, query_pool,
             kernel_out, cross_out, train_pick, query_pick,
             train_buf, query_buf, rows, blocks, part, terms, slab, full, mine, other, tile, crosses,
             local_sem, a2a_send, a2a_recv, rs_send, rs_recv, ag_send, ag_recv,
             pair_send, pair_recv, tile_send, tile_recv):
    g = lax.axis_index("groups")
    t = lax.axis_index("train")
    q = lax.axis_index("query")
    f = lax.axis_index("feat")
    n_pool, width = train_pool.shape
    block_rows = train_pick.shape[0]
    step = width // CHUNKS
    load_train = pltpu.make_async_copy(train_pool, train_buf, local_sem.at[CHUNKS])
    load_train.start()
    load_picks = [
        pltpu.make_async_copy(train_pick_in, train_pick, local_sem.at[CHUNKS + 1]),
        pltpu.make_async_copy(query_pick_in, query_pick, local_sem.at[CHUNKS + 2]),
    ]
    for load in load_picks:
        load.start()
    loads = []
    for c in range(CHUNKS):
        cols = pl.ds(c * step, step)
        load = pltpu.make_async_copy(query_pool.at[:, cols], query_buf.at[:, cols], local_sem.at[c])
        load.start()
        loads.append(load)

    offsets = [
        (a, b, c) for a in range(n_train) for b in range(n_query) for c in range(n_feat)
    ][1:]

    def peer(a, b, c):
        return lax.rem(t + a, n_train), lax.rem(q + b, n_query), lax.rem(f + c, n_feat)

    def device(where):
        return (g, where[0], where[1], where[2])

    def place(where):
        return (where[0] * n_query + where[1]) * n_feat + where[2]

    barrier = pltpu.get_barrier_semaphore()
    for off in offsets:
        pl.semaphore_signal(
            barrier, inc=1, device_id=device(peer(*off)), device_id_type=pl.DeviceIdType.MESH
        )

    for load in load_picks:
        load.wait()
    load_train.wait()
    for r in range(block_rows):
        named = jnp.clip(train_pick[r] - t * n_pool, 0, n_pool - 1)
        rows[r : r + 1, :] = train_buf[pl.ds(named, 1), :]
    pl.semaphore_wait(barrier, len(offsets))

    def remote(src, dst, send, recv, where):
        copy = pltpu.make_async_remote_copy(
            src_ref=src, dst_ref=dst, send_sem=send, recv_sem=recv,
            device_id=device(where), device_id_type=pl.DeviceIdType.MESH,
        )
        copy.start()
        return copy

    share = width // (n_train * n_query)
    a2a = []
    for a in range(1, n_train):
        where = peer(a, 0, 0)
        cols = pl.ds(pl.multiple_of((where[0] * n_query + q) * share, share), share)
        a2a.append(remote(rows.at[:, cols], blocks.at[t], a2a_send.at[a], a2a_recv.at[a], where))
    cols = pl.ds(pl.multiple_of((t * n_query + q) * share, share), share)
    blocks[t] = rows[:, cols]

    total = None
    for c in range(CHUNKS):
        loads[c].wait()
        term = dot_nt(rows[:, c * step : (c + 1) * step], query_buf[:, c * step : (c + 1) * step])
        total = term if total is None else total + term
    n_query_pool = query_pool.shape[0]
    n_queries = query_pick.shape[1]
    chosen = (
        lax.broadcasted_iota(jnp.int32, (n_query_pool, n_queries), 0)
        == query_pick[...] - q * n_query_pool
    ).astype(jnp.float32)
    mine[...] = jnp.dot(total, chosen, precision=HIGHEST, preferred_element_type=jnp.float32)
    pair = remote(mine, other, pair_send, pair_recv, peer(0, 0, 1))

    for copy in a2a:
        copy.wait()
    gathered = blocks[...].reshape(n_train * block_rows, share)
    part[...] = dot_nt(gathered, gathered)
    slab_rows = slab.shape[0]

    def slab_of(where):
        return pl.ds(pl.multiple_of(place(where) * slab_rows, slab_rows), slab_rows)

    here = (t, q, f)
    rs = []
    for i, off in enumerate(offsets):
        where = peer(*off)
        rs.append(remote(part.at[slab_of(where)], terms.at[i], rs_send.at[i], rs_recv.at[i], where))

    pair.wait()
    tile[...] = mine[...] + other[...]
    crosses[t] = tile[...]
    tiles = []
    for a in range(1, n_train):
        tiles.append(remote(tile, crosses.at[t], tile_send.at[a], tile_recv.at[a], peer(a, 0, 0)))

    for copy in rs:
        copy.wait()
    summed = part[slab_of(here), :]
    for i in range(len(offsets)):
        summed = summed + terms[i]
    slab[...] = summed
    full[slab_of(here), :] = summed
    ag = []
    for i, off in enumerate(offsets):
        ag.append(remote(slab, full.at[slab_of(here)], ag_send.at[i], ag_recv.at[i], peer(*off)))
    for copy in tiles:
        copy.wait()
    cross_out[...] = crosses[...].reshape(cross_out.shape)
    for copy in ag:
        copy.wait()
    kernel_out[...] = full[...]


def solve(kernel_ref, cross_ref, scores_ref, inverse):
    order = kernel_ref.shape[0]
    lane = lax.broadcasted_iota(jnp.int32, (8, order), 1)
    sub = lax.broadcasted_iota(jnp.int32, (8, order), 0)
    tiles = []
    for i in range(order // 8):
        diagonal = lane == sub + 8 * i
        tiles.append(kernel_ref[8 * i : 8 * i + 8, :] + jnp.where(diagonal, 0.5 * WIDTH, 0.0))
    for k in range(0, order, 2):
        home, r = k // 8, k % 8
        first = jnp.broadcast_to(tiles[home][r : r + 1, :], (8, order))
        second = jnp.broadcast_to(tiles[home][r + 1 : r + 2, :], (8, order))
        a = jnp.broadcast_to(first[:, k : k + 1], (8, order))
        b = jnp.broadcast_to(first[:, k + 1 : k + 2], (8, order))
        d = jnp.broadcast_to(second[:, k + 1 : k + 2], (8, order))
        inv_a = 1.0 / a
        ratio = b * inv_a
        inv_s = 1.0 / (d - b * ratio)
        at_k = lane == k
        at_k1 = lane == k + 1
        in_pair = at_k | at_k1
        first = jnp.where(in_pair, jnp.where(at_k, 1.0, 0.0), first)
        second = jnp.where(in_pair, jnp.where(at_k1, 1.0, 0.0), second)
        low = inv_s * (second - ratio * first)
        high = inv_a * first - ratio * low
        for i in range(order // 8):
            old = tiles[i]
            c0 = jnp.broadcast_to(old[:, k : k + 1], (8, order))
            c1 = jnp.broadcast_to(old[:, k + 1 : k + 2], (8, order))
            new = jnp.where(in_pair, 0.0, old) - c0 * high - c1 * low
            if i == home:
                new = jnp.where(sub == r, high, jnp.where(sub == r + 1, low, new))
            tiles[i] = new
    for i in range(order // 8):
        inverse[8 * i : 8 * i + 8, :] = tiles[i]
    columns = scores_ref.shape[0]
    start = pl.multiple_of(lax.axis_index("train") * columns, columns)
    scores_ref[...] = jnp.dot(
        inverse[pl.ds(start, columns), :], cross_ref[...],
        precision=HIGHEST, preferred_element_type=jnp.float32,
    )


def with_kernels(sizes, train_pool, query_pool, train_pick, query_pick):
    n_train, n_query, n_feat = sizes
    n_peers = n_train * n_query * n_feat
    block_rows = train_pick.shape[0]
    order = block_rows * n_train
    n_queries = query_pick.shape[0]
    width = train_pool.shape[1]
    share = width // (n_train * n_query)
    slab_rows = order // n_peers
    vmem = pl.BlockSpec(memory_space=pltpu.VMEM)
    hbm = pl.BlockSpec(memory_space=pltpu.HBM)
    f32 = jnp.float32
    dma = pltpu.SemaphoreType.DMA
    kernel, cross = pl.pallas_call(
        functools.partial(products, n_train, n_query, n_feat),
        out_shape=(
            jax.ShapeDtypeStruct((order, order), f32),
            jax.ShapeDtypeStruct((order, n_queries), f32),
        ),
        in_specs=[hbm] * 4,
        out_specs=(vmem, vmem),
        scratch_shapes=[
            pltpu.SMEM((block_rows,), jnp.int32),
            pltpu.VMEM((1, n_queries), jnp.int32),
            pltpu.VMEM(train_pool.shape, f32),
            pltpu.VMEM(query_pool.shape, f32),
            pltpu.VMEM((block_rows, width), f32),
            pltpu.VMEM((n_train, block_rows, share), f32),
            pltpu.VMEM((order, order), f32),
            pltpu.VMEM((n_peers - 1, slab_rows, order), f32),
            pltpu.VMEM((slab_rows, order), f32),
            pltpu.VMEM((order, order), f32),
            pltpu.VMEM((block_rows, n_queries), f32),
            pltpu.VMEM((block_rows, n_queries), f32),
            pltpu.VMEM((block_rows, n_queries), f32),
            pltpu.VMEM((n_train, block_rows, n_queries), f32),
            dma((CHUNKS + 3,)),
            dma((n_train,)), dma((n_train,)),
            dma((n_peers - 1,)), dma((n_peers - 1,)),
            dma((n_peers - 1,)), dma((n_peers - 1,)),
            dma, dma,
            dma((n_train,)), dma((n_train,)),
        ],
        compiler_params=pltpu.CompilerParams(
            collective_id=0, has_side_effects=True, vmem_limit_bytes=32 * 1024 * 1024
        ),
        name="products",
    )(train_pick, query_pick.reshape(1, n_queries), train_pool, query_pool)
    return pl.pallas_call(
        solve,
        out_shape=jax.ShapeDtypeStruct((block_rows, n_queries), f32),
        in_specs=[vmem, vmem],
        out_specs=vmem,
        scratch_shapes=[pltpu.VMEM((order, order), f32)],
        compiler_params=pltpu.CompilerParams(vmem_limit_bytes=32 * 1024 * 1024),
        name="solve",
    )(kernel, cross).T


def with_arrays(train_pool, query_pool, train_pick, query_pick):
    block_rows = train_pick.shape[0]
    train_index = lax.axis_index("train")
    query_index = lax.axis_index("query")
    train_rows = jnp.take(train_pool, train_pick - train_index * train_pool.shape[0], axis=0)
    query_rows = jnp.take(query_pool, query_pick - query_index * query_pool.shape[0], axis=0)
    cross_tile = dot_nt(query_rows, train_rows)
    kernel_part = dot_nt(train_rows, lax.all_gather(train_rows, "train", axis=0, tiled=True))
    cross_tile, kernel_part = lax.psum((cross_tile, kernel_part), "feat")
    kernel = lax.all_gather(kernel_part, "train", axis=0, tiled=True)
    order = kernel.shape[0]
    factor = jnp.linalg.cholesky(kernel + 0.5 * WIDTH * jnp.eye(order, dtype=jnp.float32))
    sel_rows = lax.broadcasted_iota(jnp.int32, (order, block_rows), 0)
    sel_cols = lax.broadcasted_iota(jnp.int32, (order, block_rows), 1) + train_index * block_rows
    selector = (sel_rows == sel_cols).astype(jnp.float32)
    halfway = lax.linalg.triangular_solve(factor, selector, left_side=True, lower=True)
    inverse_cols = lax.linalg.triangular_solve(
        factor, halfway, left_side=True, lower=True, transpose_a=True
    )
    return jnp.dot(
        lax.all_gather(cross_tile, "train", axis=1, tiled=True),
        inverse_cols,
        precision=HIGHEST,
        preferred_element_type=jnp.float32,
    )


def solution(mesh):
    sizes = mesh.shape["train"], mesh.shape["query"], mesh.shape["feat"]

    def on_device(train_pool, query_pool, train_pick, query_pick):
        order = train_pick.shape[0] * sizes[0]
        fits = (
            order == 128
            and order % (8 * sizes[0] * sizes[1] * sizes[2]) == 0
            and train_pool.shape[1] % (128 * sizes[0] * sizes[1]) == 0
        )
        if fits:
            return with_kernels(sizes, train_pool, query_pool, train_pick, query_pick)
        return with_arrays(train_pool, query_pool, train_pick, query_pick)

    return jax.shard_map(
        on_device,
        mesh=mesh,
        in_specs=(
            P(("groups", "train"), "feat"),
            P(("groups", "query"), "feat"),
            P(("groups", "train")),
            P(("groups", "query")),
        ),
        out_specs=P(("groups", "query"), "train"),
        check_vma=False,
    )
```

```python
import functools

import jax
import jax.numpy as jnp
from jax import lax
from jax.experimental import pallas as pl
from jax.experimental.pallas import tpu as pltpu
from jax.sharding import PartitionSpec as P

WIDTH = 8192
HIGHEST = lax.Precision.HIGHEST
NT = (((1,), (1,)), ((), ()))
CHUNKS = 4


def dot_nt(a, b):
    return lax.dot_general(a, b, NT, precision=HIGHEST, preferred_element_type=jnp.float32)


def halves(x):
    high = x.astype(jnp.bfloat16)
    return high, (x - high.astype(jnp.float32)).astype(jnp.bfloat16)


def invert(kernel_ref, inverse):
    order = kernel_ref.shape[0]
    lane = lax.broadcasted_iota(jnp.int32, (8, order), 1)
    sub = lax.broadcasted_iota(jnp.int32, (8, order), 0)
    tiles = []
    for i in range(order // 8):
        diagonal = lane == sub + 8 * i
        tiles.append(kernel_ref[8 * i : 8 * i + 8, :] + jnp.where(diagonal, 0.5 * WIDTH, 0.0))
    for k in range(0, order, 2):
        home, r = k // 8, k % 8
        first = jnp.broadcast_to(tiles[home][r : r + 1, :], (8, order))
        second = jnp.broadcast_to(tiles[home][r + 1 : r + 2, :], (8, order))
        a = jnp.broadcast_to(first[:, k : k + 1], (8, order))
        b = jnp.broadcast_to(first[:, k + 1 : k + 2], (8, order))
        d = jnp.broadcast_to(second[:, k + 1 : k + 2], (8, order))
        scale = 1.0 / (a * d - b * b)
        a, b, d = a * scale, b * scale, d * scale
        at_k = lane == k
        at_k1 = lane == k + 1
        in_pair = at_k | at_k1
        first = jnp.where(in_pair, jnp.where(at_k, 1.0, 0.0), first)
        second = jnp.where(in_pair, jnp.where(at_k1, 1.0, 0.0), second)
        high = d * first - b * second
        low = a * second - b * first
        following = min(k + 2, order - 1) // 8
        for i in sorted(range(order // 8), key=lambda i: i != following):
            old = tiles[i]
            c0 = jnp.broadcast_to(old[:, k : k + 1], (8, order))
            c1 = jnp.broadcast_to(old[:, k + 1 : k + 2], (8, order))
            new = jnp.where(in_pair, 0.0, old) - c0 * high - c1 * low
            if i == home:
                new = jnp.where(sub == r, high, jnp.where(sub == r + 1, low, new))
            tiles[i] = new
    for i in range(order // 8):
        inverse[8 * i : 8 * i + 8, :] = tiles[i]


def products(n_train, n_query, n_feat, train_pick_in, query_pick_in, train_pool, query_pool,
             scores_out, train_pick, query_pick,
             train_buf, query_buf, rows, blocks, part, terms, slab, full, inverse, mine, other, tile, crosses,
             local_sem, a2a_send, a2a_recv, rs_send, rs_recv, ag_send, ag_recv,
             pair_send, pair_recv, tile_send, tile_recv):
    g = lax.axis_index("groups")
    t = lax.axis_index("train")
    q = lax.axis_index("query")
    f = lax.axis_index("feat")
    n_pool, width = train_pool.shape
    block_rows = train_pick.shape[0]
    step = width // CHUNKS
    load_train = pltpu.make_async_copy(train_pool, train_buf, local_sem.at[CHUNKS])
    load_train.start()
    load_picks = [
        pltpu.make_async_copy(train_pick_in, train_pick, local_sem.at[CHUNKS + 1]),
        pltpu.make_async_copy(query_pick_in, query_pick, local_sem.at[CHUNKS + 2]),
    ]
    for load in load_picks:
        load.start()
    loads = []
    for c in range(CHUNKS):
        cols = pl.ds(c * step, step)
        load = pltpu.make_async_copy(query_pool.at[:, cols], query_buf.at[:, cols], local_sem.at[c])
        load.start()
        loads.append(load)

    offsets = [
        (a, b, c) for a in range(n_train) for b in range(n_query) for c in range(n_feat)
    ][1:]

    def peer(a, b, c):
        return lax.rem(t + a, n_train), lax.rem(q + b, n_query), lax.rem(f + c, n_feat)

    def device(where):
        return (g, where[0], where[1], where[2])

    def place(where):
        return (where[0] * n_query + where[1]) * n_feat + where[2]

    barrier = pltpu.get_barrier_semaphore()
    for off in offsets:
        pl.semaphore_signal(
            barrier, inc=1, device_id=device(peer(*off)), device_id_type=pl.DeviceIdType.MESH
        )

    for load in load_picks:
        load.wait()
    load_train.wait()
    for r in range(block_rows):
        named = jnp.clip(train_pick[r] - t * n_pool, 0, n_pool - 1)
        rows[r : r + 1, :] = train_buf[pl.ds(named, 1), :]
    pl.semaphore_wait(barrier, len(offsets))

    def remote(src, dst, send, recv, where):
        copy = pltpu.make_async_remote_copy(
            src_ref=src, dst_ref=dst, send_sem=send, recv_sem=recv,
            device_id=device(where), device_id_type=pl.DeviceIdType.MESH,
        )
        copy.start()
        return copy

    share = width // (n_train * n_query)
    a2a = []
    for a in range(1, n_train):
        where = peer(a, 0, 0)
        cols = pl.ds(pl.multiple_of((where[0] * n_query + q) * share, share), share)
        a2a.append(remote(rows.at[:, cols], blocks.at[t], a2a_send.at[a], a2a_recv.at[a], where))
    cols = pl.ds(pl.multiple_of((t * n_query + q) * share, share), share)
    blocks[t] = rows[:, cols]

    total = None
    for c in range(CHUNKS):
        loads[c].wait()
        cols = slice(c * step, (c + 1) * step)
        x_high, x_low = halves(rows[:, cols])
        y_high, y_low = halves(query_buf[:, cols])
        both = lax.dot_general(
            jnp.concatenate([x_high, x_low]), y_high, NT, preferred_element_type=jnp.float32
        )
        term = both[:block_rows] + (
            both[block_rows:]
            + lax.dot_general(x_high, y_low, NT, preferred_element_type=jnp.float32)
        )
        total = term if total is None else total + term
    n_query_pool = query_pool.shape[0]
    n_queries = query_pick.shape[1]
    chosen = (
        lax.broadcasted_iota(jnp.int32, (n_query_pool, n_queries), 0)
        == query_pick[...] - q * n_query_pool
    ).astype(jnp.float32)
    mine[...] = jnp.dot(total, chosen, precision=HIGHEST, preferred_element_type=jnp.float32)
    pair = remote(mine, other, pair_send, pair_recv, peer(0, 0, 1))

    for copy in a2a:
        copy.wait()
    gathered = blocks[...].reshape(n_train * block_rows, share)
    part[...] = dot_nt(gathered, gathered)
    slab_rows = slab.shape[0]

    def slab_of(where):
        return pl.ds(pl.multiple_of(place(where) * slab_rows, slab_rows), slab_rows)

    here = (t, q, f)
    rs = []
    for i, off in enumerate(offsets):
        where = peer(*off)
        rs.append(remote(part.at[slab_of(where)], terms.at[i], rs_send.at[i], rs_recv.at[i], where))

    pair.wait()
    tile[...] = mine[...] + other[...]
    crosses[t] = tile[...]
    tiles = []
    for a in range(1, n_train):
        tiles.append(remote(tile, crosses.at[t], tile_send.at[a], tile_recv.at[a], peer(a, 0, 0)))

    for copy in rs:
        copy.wait()
    summed = part[slab_of(here), :]
    for i in range(len(offsets)):
        summed = summed + terms[i]
    slab[...] = summed
    full[slab_of(here), :] = summed
    ag = []
    for i, off in enumerate(offsets):
        ag.append(remote(slab, full.at[slab_of(here)], ag_send.at[i], ag_recv.at[i], peer(*off)))
    for copy in ag:
        copy.wait()
    invert(full, inverse)
    for copy in tiles:
        copy.wait()
    start = pl.multiple_of(t * block_rows, block_rows)
    scores_out[...] = jnp.dot(
        inverse[pl.ds(start, block_rows), :],
        crosses[...].reshape(n_train * block_rows, n_queries),
        precision=HIGHEST,
        preferred_element_type=jnp.float32,
    )


def with_kernels(sizes, train_pool, query_pool, train_pick, query_pick):
    n_train, n_query, n_feat = sizes
    n_peers = n_train * n_query * n_feat
    block_rows = train_pick.shape[0]
    order = block_rows * n_train
    n_queries = query_pick.shape[0]
    width = train_pool.shape[1]
    share = width // (n_train * n_query)
    slab_rows = order // n_peers
    vmem = pl.BlockSpec(memory_space=pltpu.VMEM)
    hbm = pl.BlockSpec(memory_space=pltpu.HBM)
    f32 = jnp.float32
    dma = pltpu.SemaphoreType.DMA
    scores = pl.pallas_call(
        functools.partial(products, n_train, n_query, n_feat),
        out_shape=jax.ShapeDtypeStruct((block_rows, n_queries), f32),
        in_specs=[hbm] * 4,
        out_specs=vmem,
        scratch_shapes=[
            pltpu.SMEM((block_rows,), jnp.int32),
            pltpu.VMEM((1, n_queries), jnp.int32),
            pltpu.VMEM(train_pool.shape, f32),
            pltpu.VMEM(query_pool.shape, f32),
            pltpu.VMEM((block_rows, width), f32),
            pltpu.VMEM((n_train, block_rows, share), f32),
            pltpu.VMEM((order, order), f32),
            pltpu.VMEM((n_peers - 1, slab_rows, order), f32),
            pltpu.VMEM((slab_rows, order), f32),
            pltpu.VMEM((order, order), f32),
            pltpu.VMEM((order, order), f32),
            pltpu.VMEM((block_rows, n_queries), f32),
            pltpu.VMEM((block_rows, n_queries), f32),
            pltpu.VMEM((block_rows, n_queries), f32),
            pltpu.VMEM((n_train, block_rows, n_queries), f32),
            dma((CHUNKS + 3,)),
            dma((n_train,)), dma((n_train,)),
            dma((n_peers - 1,)), dma((n_peers - 1,)),
            dma((n_peers - 1,)), dma((n_peers - 1,)),
            dma, dma,
            dma((n_train,)), dma((n_train,)),
        ],
        compiler_params=pltpu.CompilerParams(
            collective_id=0, has_side_effects=True, vmem_limit_bytes=64 * 1024 * 1024
        ),
        name="products",
    )(train_pick, query_pick.reshape(1, n_queries), train_pool, query_pool)
    return scores.T


def with_arrays(train_pool, query_pool, train_pick, query_pick):
    block_rows = train_pick.shape[0]
    train_index = lax.axis_index("train")
    query_index = lax.axis_index("query")
    train_rows = jnp.take(train_pool, train_pick - train_index * train_pool.shape[0], axis=0)
    query_rows = jnp.take(query_pool, query_pick - query_index * query_pool.shape[0], axis=0)
    cross_tile = dot_nt(query_rows, train_rows)
    kernel_part = dot_nt(train_rows, lax.all_gather(train_rows, "train", axis=0, tiled=True))
    cross_tile, kernel_part = lax.psum((cross_tile, kernel_part), "feat")
    kernel = lax.all_gather(kernel_part, "train", axis=0, tiled=True)
    order = kernel.shape[0]
    factor = jnp.linalg.cholesky(kernel + 0.5 * WIDTH * jnp.eye(order, dtype=jnp.float32))
    sel_rows = lax.broadcasted_iota(jnp.int32, (order, block_rows), 0)
    sel_cols = lax.broadcasted_iota(jnp.int32, (order, block_rows), 1) + train_index * block_rows
    selector = (sel_rows == sel_cols).astype(jnp.float32)
    halfway = lax.linalg.triangular_solve(factor, selector, left_side=True, lower=True)
    inverse_cols = lax.linalg.triangular_solve(
        factor, halfway, left_side=True, lower=True, transpose_a=True
    )
    return jnp.dot(
        lax.all_gather(cross_tile, "train", axis=1, tiled=True),
        inverse_cols,
        precision=HIGHEST,
        preferred_element_type=jnp.float32,
    )


def solution(mesh):
    sizes = mesh.shape["train"], mesh.shape["query"], mesh.shape["feat"]

    def on_device(train_pool, query_pool, train_pick, query_pick):
        order = train_pick.shape[0] * sizes[0]
        fits = (
            order == 128
            and order % (8 * sizes[0] * sizes[1] * sizes[2]) == 0
            and train_pool.shape[1] % (128 * sizes[0] * sizes[1]) == 0
        )
        if fits:
            return with_kernels(sizes, train_pool, query_pool, train_pick, query_pick)
        return with_arrays(train_pool, query_pool, train_pick, query_pick)

    return jax.shard_map(
        on_device,
        mesh=mesh,
        in_specs=(
            P(("groups", "train"), "feat"),
            P(("groups", "query"), "feat"),
            P(("groups", "train")),
            P(("groups", "query")),
        ),
        out_specs=P(("groups", "query"), "train"),
        check_vma=False,
    )
```

```python
import functools

import jax
import jax.numpy as jnp
from jax import lax
from jax.experimental import pallas as pl
from jax.experimental.pallas import tpu as pltpu
from jax.sharding import PartitionSpec as P

WIDTH = 8192
HIGHEST = lax.Precision.HIGHEST
NT = (((1,), (1,)), ((), ()))
CHUNKS = 4


def dot_nt(a, b):
    return lax.dot_general(a, b, NT, precision=HIGHEST, preferred_element_type=jnp.float32)


def parts(x):
    high = x.astype(jnp.bfloat16)
    rest = x - high.astype(jnp.float32)
    middle = rest.astype(jnp.bfloat16)
    low = (rest - middle.astype(jnp.float32)).astype(jnp.bfloat16)
    return high, middle, low


def inverse_2x2(a, b, d):
    scale = 1.0 / (a * d - b * b)
    return d * scale, -b * scale, a * scale


def invert(kernel_ref, inverse):
    order = kernel_ref.shape[0]
    lane = lax.broadcasted_iota(jnp.int32, (8, order), 1)
    sub = lax.broadcasted_iota(jnp.int32, (8, order), 0)
    tiles = []
    for i in range(order // 8):
        diagonal = lane == sub + 8 * i
        tiles.append(kernel_ref[8 * i : 8 * i + 8, :] + jnp.where(diagonal, 0.5 * WIDTH, 0.0))

    def columns(tile, k):
        return [jnp.broadcast_to(tile[:, k + j : k + j + 1], (8, order)) for j in range(4)]

    def row(tile, r):
        return jnp.broadcast_to(tile[r : r + 1, :], (8, order))

    for k in range(0, order, 4):
        home, r = k // 8, k % 8
        pivots = columns(tiles[home], k)
        a00, a01, a02, a03 = (row(pivots[j], r) for j in range(4))
        a11, a12, a13 = (row(pivots[j], r + 1) for j in range(1, 4))
        a22, a23 = (row(pivots[j], r + 2) for j in range(2, 4))
        a33 = row(pivots[3], r + 3)
        in_pivot = (lane >= k) & (lane < k + 4)
        r0, r1, r2, r3 = (
            jnp.where(in_pivot, jnp.where(lane == k + j, 1.0, 0.0), row(tiles[home], r + j))
            for j in range(4)
        )
        d00, d01, d11 = inverse_2x2(a00, a01, a11)
        x00, x01 = d00 * a02 + d01 * a12, d00 * a03 + d01 * a13
        x10, x11 = d01 * a02 + d11 * a12, d01 * a03 + d11 * a13
        e00, e01, e11 = inverse_2x2(
            a22 - (a02 * x00 + a12 * x10),
            a23 - (a02 * x01 + a12 * x11),
            a33 - (a03 * x01 + a13 * x11),
        )
        v2 = r2 - (x00 * r0 + x10 * r1)
        v3 = r3 - (x01 * r0 + x11 * r1)
        w2 = e00 * v2 + e01 * v3
        w3 = e01 * v2 + e11 * v3
        w0 = (d00 * r0 + d01 * r1) - (x00 * w2 + x01 * w3)
        w1 = (d01 * r0 + d11 * r1) - (x10 * w2 + x11 * w3)
        following = min(k + 4, order - 1) // 8
        for i in sorted(range(order // 8), key=lambda i: i != following):
            c = pivots if i == home else columns(tiles[i], k)
            new = jnp.where(in_pivot, 0.0, tiles[i])
            new = new - ((c[0] * w0 + c[1] * w1) + (c[2] * w2 + c[3] * w3))
            if i == home:
                for j, w in enumerate((w0, w1, w2, w3)):
                    new = jnp.where(sub == r + j, w, new)
            tiles[i] = new
    for i in range(order // 8):
        inverse[8 * i : 8 * i + 8, :] = tiles[i]


def products(n_train, n_query, n_feat, train_pick_in, query_pick_in, train_pool, query_pool,
             scores_out, train_pick, query_pick,
             train_buf, query_buf, rows, blocks, part, terms, slab, full, inverse, mine, other, tile, crosses,
             local_sem, a2a_send, a2a_recv, rs_send, rs_recv, ag_send, ag_recv,
             pair_send, pair_recv, tile_send, tile_recv):
    g = lax.axis_index("groups")
    t = lax.axis_index("train")
    q = lax.axis_index("query")
    f = lax.axis_index("feat")
    n_pool, width = train_pool.shape
    block_rows = train_pick.shape[0]
    step = width // CHUNKS
    load_train = pltpu.make_async_copy(train_pool, train_buf, local_sem.at[CHUNKS])
    load_train.start()
    load_picks = [
        pltpu.make_async_copy(train_pick_in, train_pick, local_sem.at[CHUNKS + 1]),
        pltpu.make_async_copy(query_pick_in, query_pick, local_sem.at[CHUNKS + 2]),
    ]
    for load in load_picks:
        load.start()
    loads = []
    for c in range(CHUNKS):
        cols = pl.ds(c * step, step)
        load = pltpu.make_async_copy(query_pool.at[:, cols], query_buf.at[:, cols], local_sem.at[c])
        load.start()
        loads.append(load)

    offsets = [
        (a, b, c) for a in range(n_train) for b in range(n_query) for c in range(n_feat)
    ][1:]

    def peer(a, b, c):
        return lax.rem(t + a, n_train), lax.rem(q + b, n_query), lax.rem(f + c, n_feat)

    def device(where):
        return (g, where[0], where[1], where[2])

    def place(where):
        return (where[0] * n_query + where[1]) * n_feat + where[2]

    barrier = pltpu.get_barrier_semaphore()
    for off in offsets:
        pl.semaphore_signal(
            barrier, inc=1, device_id=device(peer(*off)), device_id_type=pl.DeviceIdType.MESH
        )

    for load in load_picks:
        load.wait()
    load_train.wait()
    named = [jnp.clip(train_pick[r] - t * n_pool, 0, n_pool - 1) for r in range(block_rows)]
    share = width // (n_train * n_query)

    def share_of(a, b):
        where = peer(a, b, 0)
        return pl.ds(pl.multiple_of((where[0] * n_query + where[1]) * share, share), share)

    def select(cols):
        for r in range(block_rows):
            rows[r : r + 1, cols] = train_buf[pl.ds(named[r], 1), cols]

    select(share_of(1, 0))
    pl.semaphore_wait(barrier, len(offsets))

    def remote(src, dst, send, recv, where):
        copy = pltpu.make_async_remote_copy(
            src_ref=src, dst_ref=dst, send_sem=send, recv_sem=recv,
            device_id=device(where), device_id_type=pl.DeviceIdType.MESH,
        )
        copy.start()
        return copy

    a2a = []
    for a in range(1, n_train):
        cols = share_of(a, 0)
        if a > 1:
            select(cols)
        a2a.append(
            remote(rows.at[:, cols], blocks.at[t], a2a_send.at[a], a2a_recv.at[a], peer(a, 0, 0))
        )
    select(share_of(0, 0))
    blocks[t] = rows[:, share_of(0, 0)]
    for a in range(n_train):
        for b in range(1, n_query):
            select(share_of(a, b))

    total = None
    for c in range(CHUNKS):
        loads[c].wait()
        cols = slice(c * step, (c + 1) * step)
        x = parts(rows[:, cols])
        y = parts(query_buf[:, cols])
        term = 0.0
        for p in (2, 1, 0):
            stacked = lax.dot_general(
                jnp.concatenate(x[: 3 - p]), y[p], NT, preferred_element_type=jnp.float32
            )
            for i in reversed(range(3 - p)):
                term = term + stacked[i * block_rows : (i + 1) * block_rows]
        total = term if total is None else total + term
    n_query_pool = query_pool.shape[0]
    n_queries = query_pick.shape[1]
    chosen = (
        lax.broadcasted_iota(jnp.int32, (n_query_pool, n_queries), 0)
        == query_pick[...] - q * n_query_pool
    ).astype(jnp.float32)
    mine[...] = jnp.dot(total, chosen, precision=HIGHEST, preferred_element_type=jnp.float32)
    pair = remote(mine, other, pair_send, pair_recv, peer(0, 0, 1))

    for copy in a2a:
        copy.wait()
    gathered = blocks[...].reshape(n_train * block_rows, share)
    part[...] = dot_nt(gathered, gathered)
    slab_rows = slab.shape[0]

    def slab_of(where):
        return pl.ds(pl.multiple_of(place(where) * slab_rows, slab_rows), slab_rows)

    here = (t, q, f)
    rs = []
    for i, off in enumerate(offsets):
        where = peer(*off)
        rs.append(remote(part.at[slab_of(where)], terms.at[i], rs_send.at[i], rs_recv.at[i], where))

    pair.wait()
    tile[...] = mine[...] + other[...]
    crosses[t] = tile[...]
    tiles = []
    for a in range(1, n_train):
        tiles.append(remote(tile, crosses.at[t], tile_send.at[a], tile_recv.at[a], peer(a, 0, 0)))

    for copy in rs:
        copy.wait()
    summed = part[slab_of(here), :]
    for i in range(len(offsets)):
        summed = summed + terms[i]
    slab[...] = summed
    full[slab_of(here), :] = summed
    ag = []
    for i, off in enumerate(offsets):
        ag.append(remote(slab, full.at[slab_of(here)], ag_send.at[i], ag_recv.at[i], peer(*off)))
    for copy in ag:
        copy.wait()
    invert(full, inverse)
    for copy in tiles:
        copy.wait()
    start = pl.multiple_of(t * block_rows, block_rows)
    scores_out[...] = jnp.dot(
        inverse[pl.ds(start, block_rows), :],
        crosses[...].reshape(n_train * block_rows, n_queries),
        precision=HIGHEST,
        preferred_element_type=jnp.float32,
    )


def with_kernels(sizes, train_pool, query_pool, train_pick, query_pick):
    n_train, n_query, n_feat = sizes
    n_peers = n_train * n_query * n_feat
    block_rows = train_pick.shape[0]
    order = block_rows * n_train
    n_queries = query_pick.shape[0]
    width = train_pool.shape[1]
    share = width // (n_train * n_query)
    slab_rows = order // n_peers
    vmem = pl.BlockSpec(memory_space=pltpu.VMEM)
    hbm = pl.BlockSpec(memory_space=pltpu.HBM)
    f32 = jnp.float32
    dma = pltpu.SemaphoreType.DMA
    scores = pl.pallas_call(
        functools.partial(products, n_train, n_query, n_feat),
        out_shape=jax.ShapeDtypeStruct((block_rows, n_queries), f32),
        in_specs=[hbm] * 4,
        out_specs=vmem,
        scratch_shapes=[
            pltpu.SMEM((block_rows,), jnp.int32),
            pltpu.VMEM((1, n_queries), jnp.int32),
            pltpu.VMEM(train_pool.shape, f32),
            pltpu.VMEM(query_pool.shape, f32),
            pltpu.VMEM((block_rows, width), f32),
            pltpu.VMEM((n_train, block_rows, share), f32),
            pltpu.VMEM((order, order), f32),
            pltpu.VMEM((n_peers - 1, slab_rows, order), f32),
            pltpu.VMEM((slab_rows, order), f32),
            pltpu.VMEM((order, order), f32),
            pltpu.VMEM((order, order), f32),
            pltpu.VMEM((block_rows, n_queries), f32),
            pltpu.VMEM((block_rows, n_queries), f32),
            pltpu.VMEM((block_rows, n_queries), f32),
            pltpu.VMEM((n_train, block_rows, n_queries), f32),
            dma((CHUNKS + 3,)),
            dma((n_train,)), dma((n_train,)),
            dma((n_peers - 1,)), dma((n_peers - 1,)),
            dma((n_peers - 1,)), dma((n_peers - 1,)),
            dma, dma,
            dma((n_train,)), dma((n_train,)),
        ],
        compiler_params=pltpu.CompilerParams(
            collective_id=0, has_side_effects=True, vmem_limit_bytes=64 * 1024 * 1024
        ),
        name="products",
    )(train_pick, query_pick.reshape(1, n_queries), train_pool, query_pool)
    return scores.T


def with_arrays(train_pool, query_pool, train_pick, query_pick):
    block_rows = train_pick.shape[0]
    train_index = lax.axis_index("train")
    query_index = lax.axis_index("query")
    train_rows = jnp.take(train_pool, train_pick - train_index * train_pool.shape[0], axis=0)
    query_rows = jnp.take(query_pool, query_pick - query_index * query_pool.shape[0], axis=0)
    cross_tile = dot_nt(query_rows, train_rows)
    kernel_part = dot_nt(train_rows, lax.all_gather(train_rows, "train", axis=0, tiled=True))
    cross_tile, kernel_part = lax.psum((cross_tile, kernel_part), "feat")
    kernel = lax.all_gather(kernel_part, "train", axis=0, tiled=True)
    order = kernel.shape[0]
    factor = jnp.linalg.cholesky(kernel + 0.5 * WIDTH * jnp.eye(order, dtype=jnp.float32))
    sel_rows = lax.broadcasted_iota(jnp.int32, (order, block_rows), 0)
    sel_cols = lax.broadcasted_iota(jnp.int32, (order, block_rows), 1) + train_index * block_rows
    selector = (sel_rows == sel_cols).astype(jnp.float32)
    halfway = lax.linalg.triangular_solve(factor, selector, left_side=True, lower=True)
    inverse_cols = lax.linalg.triangular_solve(
        factor, halfway, left_side=True, lower=True, transpose_a=True
    )
    return jnp.dot(
        lax.all_gather(cross_tile, "train", axis=1, tiled=True),
        inverse_cols,
        precision=HIGHEST,
        preferred_element_type=jnp.float32,
    )


def solution(mesh):
    sizes = mesh.shape["train"], mesh.shape["query"], mesh.shape["feat"]

    def on_device(train_pool, query_pool, train_pick, query_pick):
        order = train_pick.shape[0] * sizes[0]
        fits = (
            order == 128
            and order % (8 * sizes[0] * sizes[1] * sizes[2]) == 0
            and train_pool.shape[1] % (128 * sizes[0] * sizes[1]) == 0
        )
        if fits:
            return with_kernels(sizes, train_pool, query_pool, train_pick, query_pick)
        return with_arrays(train_pool, query_pool, train_pick, query_pick)

    return jax.shard_map(
        on_device,
        mesh=mesh,
        in_specs=(
            P(("groups", "train"), "feat"),
            P(("groups", "query"), "feat"),
            P(("groups", "train")),
            P(("groups", "query")),
        ),
        out_specs=P(("groups", "query"), "train"),
        check_vma=False,
    )
```

```python
import functools

import jax
import jax.numpy as jnp
from jax import lax
from jax.experimental import pallas as pl
from jax.experimental.pallas import tpu as pltpu
from jax.sharding import PartitionSpec as P

WIDTH = 8192
HIGHEST = lax.Precision.HIGHEST
NT = (((1,), (1,)), ((), ()))
CHUNKS = 4


def dot_nt(a, b):
    return lax.dot_general(a, b, NT, precision=HIGHEST, preferred_element_type=jnp.float32)


def parts(x):
    high = x.astype(jnp.bfloat16)
    rest = x - high.astype(jnp.float32)
    middle = rest.astype(jnp.bfloat16)
    low = (rest - middle.astype(jnp.float32)).astype(jnp.bfloat16)
    return high, middle, low


def inverse_2x2(a, b, d):
    scale = 1.0 / (a * d - b * b)
    return d * scale, -b * scale, a * scale


def invert(kernel_ref, inverse):
    order = kernel_ref.shape[0]
    lane = lax.broadcasted_iota(jnp.int32, (8, order), 1)
    sub = lax.broadcasted_iota(jnp.int32, (8, order), 0)
    tiles = []
    for i in range(order // 8):
        diagonal = lane == sub + 8 * i
        tiles.append(kernel_ref[8 * i : 8 * i + 8, :] + jnp.where(diagonal, 0.5 * WIDTH, 0.0))

    def columns(tile, k):
        return [jnp.broadcast_to(tile[:, k + j : k + j + 1], (8, order)) for j in range(4)]

    def row(tile, r):
        return jnp.broadcast_to(tile[r : r + 1, :], (8, order))

    for k in range(0, order, 4):
        home, r = k // 8, k % 8
        pivots = columns(tiles[home], k)
        a00, a01, a02, a03 = (row(pivots[j], r) for j in range(4))
        a11, a12, a13 = (row(pivots[j], r + 1) for j in range(1, 4))
        a22, a23 = (row(pivots[j], r + 2) for j in range(2, 4))
        a33 = row(pivots[3], r + 3)
        in_pivot = (lane >= k) & (lane < k + 4)
        r0, r1, r2, r3 = (
            jnp.where(in_pivot, jnp.where(lane == k + j, 1.0, 0.0), row(tiles[home], r + j))
            for j in range(4)
        )
        d00, d01, d11 = inverse_2x2(a00, a01, a11)
        x00, x01 = d00 * a02 + d01 * a12, d00 * a03 + d01 * a13
        x10, x11 = d01 * a02 + d11 * a12, d01 * a03 + d11 * a13
        e00, e01, e11 = inverse_2x2(
            a22 - (a02 * x00 + a12 * x10),
            a23 - (a02 * x01 + a12 * x11),
            a33 - (a03 * x01 + a13 * x11),
        )
        v2 = r2 - (x00 * r0 + x10 * r1)
        v3 = r3 - (x01 * r0 + x11 * r1)
        w2 = e00 * v2 + e01 * v3
        w3 = e01 * v2 + e11 * v3
        w0 = (d00 * r0 + d01 * r1) - (x00 * w2 + x01 * w3)
        w1 = (d01 * r0 + d11 * r1) - (x10 * w2 + x11 * w3)
        following = min(k + 4, order - 1) // 8
        for i in sorted(range(order // 8), key=lambda i: i != following):
            c = pivots if i == home else columns(tiles[i], k)
            new = jnp.where(in_pivot, 0.0, tiles[i])
            new = new - ((c[0] * w0 + c[1] * w1) + (c[2] * w2 + c[3] * w3))
            if i == home:
                for j, w in enumerate((w0, w1, w2, w3)):
                    new = jnp.where(sub == r + j, w, new)
            tiles[i] = new
    for i in range(order // 8):
        inverse[8 * i : 8 * i + 8, :] = tiles[i]


def products(n_train, n_query, n_feat, train_pick_in, query_pick_in, train_pool, query_pool,
             scores_out, train_pick, query_pick,
             train_buf, query_buf, rows, blocks, part, terms, slab, full, inverse, mine, other, tile, crosses,
             local_sem, a2a_send, a2a_recv, rs_send, rs_recv, ag_send, ag_recv,
             pair_send, pair_recv, tile_send, tile_recv):
    g = lax.axis_index("groups")
    t = lax.axis_index("train")
    q = lax.axis_index("query")
    f = lax.axis_index("feat")
    n_pool, width = train_pool.shape
    block_rows = train_pick.shape[0]
    step = width // CHUNKS
    load_train = pltpu.make_async_copy(train_pool, train_buf, local_sem.at[CHUNKS])
    load_train.start()
    load_picks = [
        pltpu.make_async_copy(train_pick_in, train_pick, local_sem.at[CHUNKS + 1]),
        pltpu.make_async_copy(query_pick_in, query_pick, local_sem.at[CHUNKS + 2]),
    ]
    for load in load_picks:
        load.start()
    offsets = [
        (a, b, c) for a in range(n_train) for b in range(n_query) for c in range(n_feat)
    ][:0:-1]

    def peer(a, b, c):
        return lax.rem(t + a, n_train), lax.rem(q + b, n_query), lax.rem(f + c, n_feat)

    def device(where):
        return (g, where[0], where[1], where[2])

    def place(where):
        return (where[0] * n_query + where[1]) * n_feat + where[2]

    barrier = pltpu.get_barrier_semaphore()
    for off in offsets:
        pl.semaphore_signal(
            barrier, inc=1, device_id=device(peer(*off)), device_id_type=pl.DeviceIdType.MESH
        )

    loads = []
    for c in range(CHUNKS):
        cols = pl.ds(c * step, step)
        load = pltpu.make_async_copy(query_pool.at[:, cols], query_buf.at[:, cols], local_sem.at[c])
        load.start()
        loads.append(load)
    for load in load_picks:
        load.wait()
    load_train.wait()
    named = [jnp.clip(train_pick[r] - t * n_pool, 0, n_pool - 1) for r in range(block_rows)]
    share = width // (n_train * n_query)

    def share_of(a, b):
        where = peer(a, b, 0)
        return pl.ds(pl.multiple_of((where[0] * n_query + where[1]) * share, share), share)

    def select(cols):
        for r in range(block_rows):
            rows[r : r + 1, cols] = train_buf[pl.ds(named[r], 1), cols]

    select(share_of(1, 0))
    pl.semaphore_wait(barrier, len(offsets))

    def remote(src, dst, send, recv, where):
        copy = pltpu.make_async_remote_copy(
            src_ref=src, dst_ref=dst, send_sem=send, recv_sem=recv,
            device_id=device(where), device_id_type=pl.DeviceIdType.MESH,
        )
        copy.start()
        return copy

    a2a = []
    for a in range(1, n_train):
        cols = share_of(a, 0)
        if a > 1:
            select(cols)
        a2a.append(
            remote(rows.at[:, cols], blocks.at[t], a2a_send.at[a], a2a_recv.at[a], peer(a, 0, 0))
        )
    select(share_of(0, 0))
    blocks[t] = rows[:, share_of(0, 0)]
    for a in range(n_train):
        for b in range(1, n_query):
            select(share_of(a, b))

    total = None
    for c in range(CHUNKS):
        loads[c].wait()
        cols = slice(c * step, (c + 1) * step)
        x = parts(rows[:, cols])
        y = parts(query_buf[:, cols])
        term = 0.0
        for p in (2, 1, 0):
            stacked = lax.dot_general(
                jnp.concatenate(x[: 3 - p]), y[p], NT, preferred_element_type=jnp.float32
            )
            for i in reversed(range(3 - p)):
                term = term + stacked[i * block_rows : (i + 1) * block_rows]
        total = term if total is None else total + term
    n_query_pool = query_pool.shape[0]
    n_queries = query_pick.shape[1]
    chosen = (
        lax.broadcasted_iota(jnp.int32, (n_query_pool, n_queries), 0)
        == query_pick[...] - q * n_query_pool
    ).astype(jnp.float32)
    mine[...] = jnp.dot(total, chosen, precision=HIGHEST, preferred_element_type=jnp.float32)
    pair = remote(mine, other, pair_send, pair_recv, peer(0, 0, 1))

    for copy in a2a:
        copy.wait()
    gathered = blocks[...].reshape(n_train * block_rows, share)
    part[...] = dot_nt(gathered, gathered)
    slab_rows = slab.shape[0]

    def slab_of(where):
        return pl.ds(pl.multiple_of(place(where) * slab_rows, slab_rows), slab_rows)

    here = (t, q, f)
    rs = []
    for i, off in enumerate(offsets):
        where = peer(*off)
        rs.append(remote(part.at[slab_of(where)], terms.at[i], rs_send.at[i], rs_recv.at[i], where))

    pair.wait()
    tile[...] = mine[...] + other[...]
    crosses[t] = tile[...]
    tiles = []
    for a in range(1, n_train):
        tiles.append(remote(tile, crosses.at[t], tile_send.at[a], tile_recv.at[a], peer(a, 0, 0)))

    for copy in rs:
        copy.wait()
    summed = part[slab_of(here), :]
    for i in range(len(offsets)):
        summed = summed + terms[i]
    slab[...] = summed
    full[slab_of(here), :] = summed
    ag = []
    for i, off in enumerate(offsets):
        ag.append(remote(slab, full.at[slab_of(here)], ag_send.at[i], ag_recv.at[i], peer(*off)))
    for copy in ag:
        copy.wait()
    invert(full, inverse)
    for copy in tiles:
        copy.wait()
    start = pl.multiple_of(t * block_rows, block_rows)
    scores_out[...] = jnp.dot(
        inverse[pl.ds(start, block_rows), :],
        crosses[...].reshape(n_train * block_rows, n_queries),
        precision=HIGHEST,
        preferred_element_type=jnp.float32,
    )


def with_kernels(sizes, train_pool, query_pool, train_pick, query_pick):
    n_train, n_query, n_feat = sizes
    n_peers = n_train * n_query * n_feat
    block_rows = train_pick.shape[0]
    order = block_rows * n_train
    n_queries = query_pick.shape[0]
    width = train_pool.shape[1]
    share = width // (n_train * n_query)
    slab_rows = order // n_peers
    vmem = pl.BlockSpec(memory_space=pltpu.VMEM)
    hbm = pl.BlockSpec(memory_space=pltpu.HBM)
    f32 = jnp.float32
    dma = pltpu.SemaphoreType.DMA
    scores = pl.pallas_call(
        functools.partial(products, n_train, n_query, n_feat),
        out_shape=jax.ShapeDtypeStruct((block_rows, n_queries), f32),
        in_specs=[hbm] * 4,
        out_specs=vmem,
        scratch_shapes=[
            pltpu.SMEM((block_rows,), jnp.int32),
            pltpu.VMEM((1, n_queries), jnp.int32),
            pltpu.VMEM(train_pool.shape, f32),
            pltpu.VMEM(query_pool.shape, f32),
            pltpu.VMEM((block_rows, width), f32),
            pltpu.VMEM((n_train, block_rows, share), f32),
            pltpu.VMEM((order, order), f32),
            pltpu.VMEM((n_peers - 1, slab_rows, order), f32),
            pltpu.VMEM((slab_rows, order), f32),
            pltpu.VMEM((order, order), f32),
            pltpu.VMEM((order, order), f32),
            pltpu.VMEM((block_rows, n_queries), f32),
            pltpu.VMEM((block_rows, n_queries), f32),
            pltpu.VMEM((block_rows, n_queries), f32),
            pltpu.VMEM((n_train, block_rows, n_queries), f32),
            dma((CHUNKS + 3,)),
            dma((n_train,)), dma((n_train,)),
            dma((n_peers - 1,)), dma((n_peers - 1,)),
            dma((n_peers - 1,)), dma((n_peers - 1,)),
            dma, dma,
            dma((n_train,)), dma((n_train,)),
        ],
        compiler_params=pltpu.CompilerParams(
            collective_id=0, has_side_effects=True, vmem_limit_bytes=64 * 1024 * 1024
        ),
        name="products",
    )(train_pick, query_pick.reshape(1, n_queries), train_pool, query_pool)
    return scores.T


def with_arrays(train_pool, query_pool, train_pick, query_pick):
    block_rows = train_pick.shape[0]
    train_index = lax.axis_index("train")
    query_index = lax.axis_index("query")
    train_rows = jnp.take(train_pool, train_pick - train_index * train_pool.shape[0], axis=0)
    query_rows = jnp.take(query_pool, query_pick - query_index * query_pool.shape[0], axis=0)
    cross_tile = dot_nt(query_rows, train_rows)
    kernel_part = dot_nt(train_rows, lax.all_gather(train_rows, "train", axis=0, tiled=True))
    cross_tile, kernel_part = lax.psum((cross_tile, kernel_part), "feat")
    kernel = lax.all_gather(kernel_part, "train", axis=0, tiled=True)
    order = kernel.shape[0]
    factor = jnp.linalg.cholesky(kernel + 0.5 * WIDTH * jnp.eye(order, dtype=jnp.float32))
    sel_rows = lax.broadcasted_iota(jnp.int32, (order, block_rows), 0)
    sel_cols = lax.broadcasted_iota(jnp.int32, (order, block_rows), 1) + train_index * block_rows
    selector = (sel_rows == sel_cols).astype(jnp.float32)
    halfway = lax.linalg.triangular_solve(factor, selector, left_side=True, lower=True)
    inverse_cols = lax.linalg.triangular_solve(
        factor, halfway, left_side=True, lower=True, transpose_a=True
    )
    return jnp.dot(
        lax.all_gather(cross_tile, "train", axis=1, tiled=True),
        inverse_cols,
        precision=HIGHEST,
        preferred_element_type=jnp.float32,
    )


def solution(mesh):
    sizes = mesh.shape["train"], mesh.shape["query"], mesh.shape["feat"]

    def on_device(train_pool, query_pool, train_pick, query_pick):
        order = train_pick.shape[0] * sizes[0]
        fits = (
            order == 128
            and order % (8 * sizes[0] * sizes[1] * sizes[2]) == 0
            and train_pool.shape[1] % (128 * sizes[0] * sizes[1]) == 0
        )
        if fits:
            return with_kernels(sizes, train_pool, query_pool, train_pick, query_pick)
        return with_arrays(train_pool, query_pool, train_pick, query_pick)

    return jax.shard_map(
        on_device,
        mesh=mesh,
        in_specs=(
            P(("groups", "train"), "feat"),
            P(("groups", "query"), "feat"),
            P(("groups", "train")),
            P(("groups", "query")),
        ),
        out_specs=P(("groups", "query"), "train"),
        check_vma=False,
    )
```

```python
import functools

import jax
import jax.numpy as jnp
from jax import lax
from jax.experimental import pallas as pl
from jax.experimental.pallas import tpu as pltpu
from jax.sharding import PartitionSpec as P

WIDTH = 8192
HIGHEST = lax.Precision.HIGHEST
NT = (((1,), (1,)), ((), ()))
CHUNKS = 4


def dot_nt(a, b):
    return lax.dot_general(a, b, NT, precision=HIGHEST, preferred_element_type=jnp.float32)


def parts(x):
    high = x.astype(jnp.bfloat16)
    rest = x - high.astype(jnp.float32)
    middle = rest.astype(jnp.bfloat16)
    low = (rest - middle.astype(jnp.float32)).astype(jnp.bfloat16)
    return high, middle, low


def inverse_2x2(a, b, d):
    scale = 1.0 / (a * d - b * b)
    return d * scale, -b * scale, a * scale


def invert(kernel_ref, inverse):
    order = kernel_ref.shape[0]
    lane = lax.broadcasted_iota(jnp.int32, (8, order), 1)
    sub = lax.broadcasted_iota(jnp.int32, (8, order), 0)
    tiles = []
    for i in range(order // 8):
        diagonal = lane == sub + 8 * i
        tiles.append(kernel_ref[8 * i : 8 * i + 8, :] + jnp.where(diagonal, 0.5 * WIDTH, 0.0))

    def columns(tile, k):
        return [jnp.broadcast_to(tile[:, k + j : k + j + 1], (8, order)) for j in range(4)]

    def row(tile, r):
        return jnp.broadcast_to(tile[r : r + 1, :], (8, order))

    for k in range(0, order, 4):
        home, r = k // 8, k % 8
        pivots = columns(tiles[home], k)
        a00, a01, a02, a03 = (row(pivots[j], r) for j in range(4))
        a11, a12, a13 = (row(pivots[j], r + 1) for j in range(1, 4))
        a22, a23 = (row(pivots[j], r + 2) for j in range(2, 4))
        a33 = row(pivots[3], r + 3)
        in_pivot = (lane >= k) & (lane < k + 4)
        r0, r1, r2, r3 = (
            jnp.where(in_pivot, jnp.where(lane == k + j, 1.0, 0.0), row(tiles[home], r + j))
            for j in range(4)
        )
        d00, d01, d11 = inverse_2x2(a00, a01, a11)
        x00, x01 = d00 * a02 + d01 * a12, d00 * a03 + d01 * a13
        x10, x11 = d01 * a02 + d11 * a12, d01 * a03 + d11 * a13
        e00, e01, e11 = inverse_2x2(
            a22 - (a02 * x00 + a12 * x10),
            a23 - (a02 * x01 + a12 * x11),
            a33 - (a03 * x01 + a13 * x11),
        )
        v2 = r2 - (x00 * r0 + x10 * r1)
        v3 = r3 - (x01 * r0 + x11 * r1)
        w2 = e00 * v2 + e01 * v3
        w3 = e01 * v2 + e11 * v3
        w0 = (d00 * r0 + d01 * r1) - (x00 * w2 + x01 * w3)
        w1 = (d01 * r0 + d11 * r1) - (x10 * w2 + x11 * w3)
        following = min(k + 4, order - 1) // 8
        for i in sorted(range(order // 8), key=lambda i: i != following):
            c = pivots if i == home else columns(tiles[i], k)
            new = jnp.where(in_pivot, 0.0, tiles[i])
            new = new - ((c[0] * w0 + c[1] * w1) + (c[2] * w2 + c[3] * w3))
            if i == home:
                for j, w in enumerate((w0, w1, w2, w3)):
                    new = jnp.where(sub == r + j, w, new)
            tiles[i] = new
    for i in range(order // 8):
        inverse[8 * i : 8 * i + 8, :] = tiles[i]


def products(n_train, n_query, n_feat, train_pick_in, query_pick_in, train_pool, query_pool,
             scores_out, train_pick, query_pick,
             train_buf, query_buf, rows, blocks, part, terms, slab, full, inverse, mine, other, tile, crosses,
             local_sem, a2a_send, a2a_recv, rs_send, rs_recv, ag_send, ag_recv,
             pair_send, pair_recv, tile_send, tile_recv):
    g = lax.axis_index("groups")
    t = lax.axis_index("train")
    q = lax.axis_index("query")
    f = lax.axis_index("feat")
    n_pool, width = train_pool.shape
    block_rows = train_pick.shape[0]
    step = width // CHUNKS
    load_train = pltpu.make_async_copy(train_pool, train_buf, local_sem.at[CHUNKS])
    load_train.start()
    load_picks = [
        pltpu.make_async_copy(train_pick_in, train_pick, local_sem.at[CHUNKS + 1]),
        pltpu.make_async_copy(query_pick_in, query_pick, local_sem.at[CHUNKS + 2]),
    ]
    for load in load_picks:
        load.start()
    offsets = [
        (a, b, c) for a in range(n_train) for b in range(n_query) for c in range(n_feat)
    ][:0:-1]

    def peer(a, b, c):
        return lax.rem(t + a, n_train), lax.rem(q + b, n_query), lax.rem(f + c, n_feat)

    def device(where):
        return (g, where[0], where[1], where[2])

    def place(where):
        return (where[0] * n_query + where[1]) * n_feat + where[2]

    barrier = pltpu.get_barrier_semaphore()
    for off in offsets:
        pl.semaphore_signal(
            barrier, inc=1, device_id=device(peer(*off)), device_id_type=pl.DeviceIdType.MESH
        )

    loads = []
    for c in range(CHUNKS):
        cols = pl.ds(c * step, step)
        load = pltpu.make_async_copy(query_pool.at[:, cols], query_buf.at[:, cols], local_sem.at[c])
        load.start()
        loads.append(load)
    for load in load_picks:
        load.wait()
    load_train.wait()
    named = [jnp.clip(train_pick[r] - t * n_pool, 0, n_pool - 1) for r in range(block_rows)]
    share = width // (n_train * n_query)

    def share_of(a, b):
        where = peer(a, b, 0)
        return pl.ds(pl.multiple_of((where[0] * n_query + where[1]) * share, share), share)

    def select(cols):
        for r in range(block_rows):
            rows[r : r + 1, cols] = train_buf[pl.ds(named[r], 1), cols]

    select(share_of(1, 0))
    pl.semaphore_wait(barrier, len(offsets))

    def remote(src, dst, send, recv, where):
        copy = pltpu.make_async_remote_copy(
            src_ref=src, dst_ref=dst, send_sem=send, recv_sem=recv,
            device_id=device(where), device_id_type=pl.DeviceIdType.MESH,
        )
        copy.start()
        return copy

    a2a = []
    for a in range(1, n_train):
        cols = share_of(a, 0)
        if a > 1:
            select(cols)
        a2a.append(
            remote(rows.at[:, cols], blocks.at[t], a2a_send.at[a], a2a_recv.at[a], peer(a, 0, 0))
        )
    select(share_of(0, 0))
    blocks[t] = rows[:, share_of(0, 0)]
    for a in range(n_train):
        for b in range(1, n_query):
            select(share_of(a, b))

    total = None
    for c in range(CHUNKS):
        loads[c].wait()
        cols = slice(c * step, (c + 1) * step)
        x = parts(rows[:, cols])
        y = parts(query_buf[:, cols])
        term = 0.0
        for p in (2, 1, 0):
            stacked = lax.dot_general(
                jnp.concatenate(x[: 3 - p]), y[p], NT, preferred_element_type=jnp.float32
            )
            for i in reversed(range(3 - p)):
                term = term + stacked[i * block_rows : (i + 1) * block_rows]
        total = term if total is None else total + term
    n_query_pool = query_pool.shape[0]
    n_queries = query_pick.shape[1]
    chosen = (
        lax.broadcasted_iota(jnp.int32, (n_query_pool, n_queries), 0)
        == query_pick[...] - q * n_query_pool
    ).astype(jnp.float32)
    mine[...] = jnp.dot(total, chosen, precision=HIGHEST, preferred_element_type=jnp.float32)
    pair = remote(mine, other, pair_send, pair_recv, peer(0, 0, 1))

    for copy in a2a:
        copy.wait()
    gathered = blocks[...].reshape(n_train * block_rows, share)
    part[...] = dot_nt(gathered, gathered)
    slab_rows = slab.shape[0]

    def slab_of(where):
        return pl.ds(pl.multiple_of(place(where) * slab_rows, slab_rows), slab_rows)

    here = (t, q, f)
    rs = []
    for i, off in enumerate(offsets):
        where = peer(*off)
        rs.append(remote(part.at[slab_of(where)], terms.at[i], rs_send.at[i], rs_recv.at[i], where))

    for copy in rs:
        copy.wait()
    summed = part[slab_of(here), :]
    for i in range(len(offsets)):
        summed = summed + terms[i]
    slab[...] = summed
    full[slab_of(here), :] = summed
    ag = []
    for i, off in enumerate(offsets):
        ag.append(remote(slab, full.at[slab_of(here)], ag_send.at[i], ag_recv.at[i], peer(*off)))
    pair.wait()
    tile[...] = mine[...] + other[...]
    crosses[t] = tile[...]
    tiles = []
    for a in range(1, n_train):
        tiles.append(remote(tile, crosses.at[t], tile_send.at[a], tile_recv.at[a], peer(a, 0, 0)))

    for copy in ag:
        copy.wait()
    invert(full, inverse)
    for copy in tiles:
        copy.wait()
    start = pl.multiple_of(t * block_rows, block_rows)
    scores_out[...] = jnp.dot(
        inverse[pl.ds(start, block_rows), :],
        crosses[...].reshape(n_train * block_rows, n_queries),
        precision=HIGHEST,
        preferred_element_type=jnp.float32,
    )


def with_kernels(sizes, train_pool, query_pool, train_pick, query_pick):
    n_train, n_query, n_feat = sizes
    n_peers = n_train * n_query * n_feat
    block_rows = train_pick.shape[0]
    order = block_rows * n_train
    n_queries = query_pick.shape[0]
    width = train_pool.shape[1]
    share = width // (n_train * n_query)
    slab_rows = order // n_peers
    vmem = pl.BlockSpec(memory_space=pltpu.VMEM)
    hbm = pl.BlockSpec(memory_space=pltpu.HBM)
    f32 = jnp.float32
    dma = pltpu.SemaphoreType.DMA
    scores = pl.pallas_call(
        functools.partial(products, n_train, n_query, n_feat),
        out_shape=jax.ShapeDtypeStruct((block_rows, n_queries), f32),
        in_specs=[hbm] * 4,
        out_specs=vmem,
        scratch_shapes=[
            pltpu.SMEM((block_rows,), jnp.int32),
            pltpu.VMEM((1, n_queries), jnp.int32),
            pltpu.VMEM(train_pool.shape, f32),
            pltpu.VMEM(query_pool.shape, f32),
            pltpu.VMEM((block_rows, width), f32),
            pltpu.VMEM((n_train, block_rows, share), f32),
            pltpu.VMEM((order, order), f32),
            pltpu.VMEM((n_peers - 1, slab_rows, order), f32),
            pltpu.VMEM((slab_rows, order), f32),
            pltpu.VMEM((order, order), f32),
            pltpu.VMEM((order, order), f32),
            pltpu.VMEM((block_rows, n_queries), f32),
            pltpu.VMEM((block_rows, n_queries), f32),
            pltpu.VMEM((block_rows, n_queries), f32),
            pltpu.VMEM((n_train, block_rows, n_queries), f32),
            dma((CHUNKS + 3,)),
            dma((n_train,)), dma((n_train,)),
            dma((n_peers - 1,)), dma((n_peers - 1,)),
            dma((n_peers - 1,)), dma((n_peers - 1,)),
            dma, dma,
            dma((n_train,)), dma((n_train,)),
        ],
        compiler_params=pltpu.CompilerParams(
            collective_id=0, has_side_effects=True, vmem_limit_bytes=64 * 1024 * 1024
        ),
        name="products",
    )(train_pick, query_pick.reshape(1, n_queries), train_pool, query_pool)
    return scores.T


def with_arrays(train_pool, query_pool, train_pick, query_pick):
    block_rows = train_pick.shape[0]
    train_index = lax.axis_index("train")
    query_index = lax.axis_index("query")
    train_rows = jnp.take(train_pool, train_pick - train_index * train_pool.shape[0], axis=0)
    query_rows = jnp.take(query_pool, query_pick - query_index * query_pool.shape[0], axis=0)
    cross_tile = dot_nt(query_rows, train_rows)
    kernel_part = dot_nt(train_rows, lax.all_gather(train_rows, "train", axis=0, tiled=True))
    cross_tile, kernel_part = lax.psum((cross_tile, kernel_part), "feat")
    kernel = lax.all_gather(kernel_part, "train", axis=0, tiled=True)
    order = kernel.shape[0]
    factor = jnp.linalg.cholesky(kernel + 0.5 * WIDTH * jnp.eye(order, dtype=jnp.float32))
    sel_rows = lax.broadcasted_iota(jnp.int32, (order, block_rows), 0)
    sel_cols = lax.broadcasted_iota(jnp.int32, (order, block_rows), 1) + train_index * block_rows
    selector = (sel_rows == sel_cols).astype(jnp.float32)
    halfway = lax.linalg.triangular_solve(factor, selector, left_side=True, lower=True)
    inverse_cols = lax.linalg.triangular_solve(
        factor, halfway, left_side=True, lower=True, transpose_a=True
    )
    return jnp.dot(
        lax.all_gather(cross_tile, "train", axis=1, tiled=True),
        inverse_cols,
        precision=HIGHEST,
        preferred_element_type=jnp.float32,
    )


def solution(mesh):
    sizes = mesh.shape["train"], mesh.shape["query"], mesh.shape["feat"]

    def on_device(train_pool, query_pool, train_pick, query_pick):
        order = train_pick.shape[0] * sizes[0]
        fits = (
            order == 128
            and order % (8 * sizes[0] * sizes[1] * sizes[2]) == 0
            and train_pool.shape[1] % (128 * sizes[0] * sizes[1]) == 0
        )
        if fits:
            return with_kernels(sizes, train_pool, query_pool, train_pick, query_pick)
        return with_arrays(train_pool, query_pool, train_pick, query_pick)

    return jax.shard_map(
        on_device,
        mesh=mesh,
        in_specs=(
            P(("groups", "train"), "feat"),
            P(("groups", "query"), "feat"),
            P(("groups", "train")),
            P(("groups", "query")),
        ),
        out_specs=P(("groups", "query"), "train"),
        check_vma=False,
    )
```

```python
import functools

import jax
import jax.numpy as jnp
from jax import lax
from jax.experimental import pallas as pl
from jax.experimental.pallas import tpu as pltpu
from jax.sharding import PartitionSpec as P

WIDTH = 8192
HIGHEST = lax.Precision.HIGHEST
NT = (((1,), (1,)), ((), ()))
CHUNKS = 4


def dot_nt(a, b):
    return lax.dot_general(a, b, NT, precision=HIGHEST, preferred_element_type=jnp.float32)


def parts(x):
    high = x.astype(jnp.bfloat16)
    rest = x - high.astype(jnp.float32)
    middle = rest.astype(jnp.bfloat16)
    low = (rest - middle.astype(jnp.float32)).astype(jnp.bfloat16)
    return high, middle, low


def invert(kernel_ref, inverse):
    order = kernel_ref.shape[0]
    lane = lax.broadcasted_iota(jnp.int32, (8, order), 1)
    sub = lax.broadcasted_iota(jnp.int32, (8, order), 0)
    tiles = []
    for i in range(order // 8):
        diagonal = lane == sub + 8 * i
        tiles.append(kernel_ref[8 * i : 8 * i + 8, :] * (1 / WIDTH) + jnp.where(diagonal, 0.5, 0.0))

    def columns(tile, k):
        return [jnp.broadcast_to(tile[:, k + j : k + j + 1], (8, order)) for j in range(4)]

    def row(tile, r):
        return jnp.broadcast_to(tile[r : r + 1, :], (8, order))

    for k in range(0, order, 4):
        home, r = k // 8, k % 8
        pivots = columns(tiles[home], k)
        a00, a01, a02, a03 = (row(pivots[j], r) for j in range(4))
        a11, a12, a13 = (row(pivots[j], r + 1) for j in range(1, 4))
        a22, a23 = (row(pivots[j], r + 2) for j in range(2, 4))
        a33 = row(pivots[3], r + 3)
        in_pivot = (lane >= k) & (lane < k + 4)
        r0, r1, r2, r3 = (
            jnp.where(in_pivot, jnp.where(lane == k + j, 1.0, 0.0), row(tiles[home], r + j))
            for j in range(4)
        )
        det = a00 * a11 - a01 * a01
        y00, y01 = a11 * a02 - a01 * a12, a11 * a03 - a01 * a13
        y10, y11 = a00 * a12 - a01 * a02, a00 * a13 - a01 * a03
        s00 = det * a22 - (a02 * y00 + a12 * y10)
        s01 = det * a23 - (a02 * y01 + a12 * y11)
        s11 = det * a33 - (a03 * y01 + a13 * y11)
        first = 1.0 / det
        second = det * (1.0 / (s00 * s11 - s01 * s01))
        d00, d01, d11 = a11 * first, -a01 * first, a00 * first
        x00, x01, x10, x11 = y00 * first, y01 * first, y10 * first, y11 * first
        e00, e01, e11 = s11 * second, -s01 * second, s00 * second
        v2 = r2 - (x00 * r0 + x10 * r1)
        v3 = r3 - (x01 * r0 + x11 * r1)
        w2 = e00 * v2 + e01 * v3
        w3 = e01 * v2 + e11 * v3
        w0 = (d00 * r0 + d01 * r1) - (x00 * w2 + x01 * w3)
        w1 = (d01 * r0 + d11 * r1) - (x10 * w2 + x11 * w3)
        following = min(k + 4, order - 1) // 8
        for i in sorted(range(order // 8), key=lambda i: i != following):
            c = pivots if i == home else columns(tiles[i], k)
            new = jnp.where(in_pivot, 0.0, tiles[i])
            new = new - ((c[0] * w0 + c[1] * w1) + (c[2] * w2 + c[3] * w3))
            if i == home:
                for j, w in enumerate((w0, w1, w2, w3)):
                    new = jnp.where(sub == r + j, w, new)
            tiles[i] = new
    for i in range(order // 8):
        inverse[8 * i : 8 * i + 8, :] = tiles[i] * (1 / WIDTH)


def products(n_train, n_query, n_feat, train_pick_in, query_pick_in, train_pool, query_pool,
             scores_out, train_pick, query_pick,
             train_buf, query_buf, rows, blocks, part, terms, slab, full, inverse, mine, other, tile, crosses,
             local_sem, a2a_send, a2a_recv, rs_send, rs_recv, ag_send, ag_recv,
             pair_send, pair_recv, tile_send, tile_recv):
    g = lax.axis_index("groups")
    t = lax.axis_index("train")
    q = lax.axis_index("query")
    f = lax.axis_index("feat")
    n_pool, width = train_pool.shape
    block_rows = train_pick.shape[0]
    step = width // CHUNKS
    load_train = pltpu.make_async_copy(train_pool, train_buf, local_sem.at[CHUNKS])
    load_train.start()
    load_picks = [
        pltpu.make_async_copy(train_pick_in, train_pick, local_sem.at[CHUNKS + 1]),
        pltpu.make_async_copy(query_pick_in, query_pick, local_sem.at[CHUNKS + 2]),
    ]
    for load in load_picks:
        load.start()
    offsets = [
        (a, b, c) for a in range(n_train) for b in range(n_query) for c in range(n_feat)
    ][:0:-1]

    def peer(a, b, c):
        return lax.rem(t + a, n_train), lax.rem(q + b, n_query), lax.rem(f + c, n_feat)

    def device(where):
        return (g, where[0], where[1], where[2])

    def place(where):
        return (where[0] * n_query + where[1]) * n_feat + where[2]

    barrier = pltpu.get_barrier_semaphore()
    for off in offsets:
        pl.semaphore_signal(
            barrier, inc=1, device_id=device(peer(*off)), device_id_type=pl.DeviceIdType.MESH
        )

    loads = []
    for c in range(CHUNKS):
        cols = pl.ds(c * step, step)
        load = pltpu.make_async_copy(query_pool.at[:, cols], query_buf.at[:, cols], local_sem.at[c])
        load.start()
        loads.append(load)
    for load in load_picks:
        load.wait()
    load_train.wait()
    named = [jnp.clip(train_pick[r] - t * n_pool, 0, n_pool - 1) for r in range(block_rows)]
    share = width // (n_train * n_query)

    def share_of(a, b):
        where = peer(a, b, 0)
        return pl.ds(pl.multiple_of((where[0] * n_query + where[1]) * share, share), share)

    def select(cols):
        for r in range(block_rows):
            rows[r : r + 1, cols] = train_buf[pl.ds(named[r], 1), cols]

    select(share_of(1, 0))
    pl.semaphore_wait(barrier, len(offsets))

    def remote(src, dst, send, recv, where):
        copy = pltpu.make_async_remote_copy(
            src_ref=src, dst_ref=dst, send_sem=send, recv_sem=recv,
            device_id=device(where), device_id_type=pl.DeviceIdType.MESH,
        )
        copy.start()
        return copy

    a2a = []
    for a in range(1, n_train):
        cols = share_of(a, 0)
        if a > 1:
            select(cols)
        a2a.append(
            remote(rows.at[:, cols], blocks.at[t], a2a_send.at[a], a2a_recv.at[a], peer(a, 0, 0))
        )
    select(share_of(0, 0))
    blocks[t] = rows[:, share_of(0, 0)]
    for a in range(n_train):
        for b in range(1, n_query):
            select(share_of(a, b))

    total = None
    for c in range(CHUNKS):
        loads[c].wait()
        cols = slice(c * step, (c + 1) * step)
        x = parts(rows[:, cols])
        y = parts(query_buf[:, cols])
        term = 0.0
        for p in (2, 1, 0):
            stacked = lax.dot_general(
                jnp.concatenate(x[: 3 - p]), y[p], NT, preferred_element_type=jnp.float32
            )
            for i in reversed(range(3 - p)):
                term = term + stacked[i * block_rows : (i + 1) * block_rows]
        total = term if total is None else total + term
    n_query_pool = query_pool.shape[0]
    n_queries = query_pick.shape[1]
    chosen = (
        lax.broadcasted_iota(jnp.int32, (n_query_pool, n_queries), 0)
        == query_pick[...] - q * n_query_pool
    ).astype(jnp.float32)
    mine[...] = jnp.dot(total, chosen, precision=HIGHEST, preferred_element_type=jnp.float32)
    pair = remote(mine, other, pair_send, pair_recv, peer(0, 0, 1))

    for copy in a2a:
        copy.wait()
    gathered = blocks[...].reshape(n_train * block_rows, share)
    part[...] = dot_nt(gathered, gathered)
    slab_rows = slab.shape[0]

    def slab_of(where):
        return pl.ds(pl.multiple_of(place(where) * slab_rows, slab_rows), slab_rows)

    here = (t, q, f)
    rs = []
    for i, off in enumerate(offsets):
        where = peer(*off)
        rs.append(remote(part.at[slab_of(where)], terms.at[i], rs_send.at[i], rs_recv.at[i], where))

    pair.wait()
    tile[...] = mine[...] + other[...]
    crosses[t] = tile[...]
    tiles = []
    for a in range(1, n_train):
        tiles.append(remote(tile, crosses.at[t], tile_send.at[a], tile_recv.at[a], peer(a, 0, 0)))

    for copy in rs:
        copy.wait()
    summed = part[slab_of(here), :]
    for i in range(len(offsets)):
        summed = summed + terms[i]
    slab[...] = summed
    full[slab_of(here), :] = summed
    ag = []
    for i, off in enumerate(offsets):
        ag.append(remote(slab, full.at[slab_of(here)], ag_send.at[i], ag_recv.at[i], peer(*off)))
    for copy in ag:
        copy.wait()
    invert(full, inverse)
    for copy in tiles:
        copy.wait()
    start = pl.multiple_of(t * block_rows, block_rows)
    scores_out[...] = jnp.dot(
        inverse[pl.ds(start, block_rows), :],
        crosses[...].reshape(n_train * block_rows, n_queries),
        precision=HIGHEST,
        preferred_element_type=jnp.float32,
    )


def with_kernels(sizes, train_pool, query_pool, train_pick, query_pick):
    n_train, n_query, n_feat = sizes
    n_peers = n_train * n_query * n_feat
    block_rows = train_pick.shape[0]
    order = block_rows * n_train
    n_queries = query_pick.shape[0]
    width = train_pool.shape[1]
    share = width // (n_train * n_query)
    slab_rows = order // n_peers
    vmem = pl.BlockSpec(memory_space=pltpu.VMEM)
    hbm = pl.BlockSpec(memory_space=pltpu.HBM)
    f32 = jnp.float32
    dma = pltpu.SemaphoreType.DMA
    scores = pl.pallas_call(
        functools.partial(products, n_train, n_query, n_feat),
        out_shape=jax.ShapeDtypeStruct((block_rows, n_queries), f32),
        in_specs=[hbm] * 4,
        out_specs=vmem,
        scratch_shapes=[
            pltpu.SMEM((block_rows,), jnp.int32),
            pltpu.VMEM((1, n_queries), jnp.int32),
            pltpu.VMEM(train_pool.shape, f32),
            pltpu.VMEM(query_pool.shape, f32),
            pltpu.VMEM((block_rows, width), f32),
            pltpu.VMEM((n_train, block_rows, share), f32),
            pltpu.VMEM((order, order), f32),
            pltpu.VMEM((n_peers - 1, slab_rows, order), f32),
            pltpu.VMEM((slab_rows, order), f32),
            pltpu.VMEM((order, order), f32),
            pltpu.VMEM((order, order), f32),
            pltpu.VMEM((block_rows, n_queries), f32),
            pltpu.VMEM((block_rows, n_queries), f32),
            pltpu.VMEM((block_rows, n_queries), f32),
            pltpu.VMEM((n_train, block_rows, n_queries), f32),
            dma((CHUNKS + 3,)),
            dma((n_train,)), dma((n_train,)),
            dma((n_peers - 1,)), dma((n_peers - 1,)),
            dma((n_peers - 1,)), dma((n_peers - 1,)),
            dma, dma,
            dma((n_train,)), dma((n_train,)),
        ],
        compiler_params=pltpu.CompilerParams(
            collective_id=0, has_side_effects=True, vmem_limit_bytes=64 * 1024 * 1024
        ),
        name="products",
    )(train_pick, query_pick.reshape(1, n_queries), train_pool, query_pool)
    return scores.T


def with_arrays(train_pool, query_pool, train_pick, query_pick):
    block_rows = train_pick.shape[0]
    train_index = lax.axis_index("train")
    query_index = lax.axis_index("query")
    train_rows = jnp.take(train_pool, train_pick - train_index * train_pool.shape[0], axis=0)
    query_rows = jnp.take(query_pool, query_pick - query_index * query_pool.shape[0], axis=0)
    cross_tile = dot_nt(query_rows, train_rows)
    kernel_part = dot_nt(train_rows, lax.all_gather(train_rows, "train", axis=0, tiled=True))
    cross_tile, kernel_part = lax.psum((cross_tile, kernel_part), "feat")
    kernel = lax.all_gather(kernel_part, "train", axis=0, tiled=True)
    order = kernel.shape[0]
    factor = jnp.linalg.cholesky(kernel + 0.5 * WIDTH * jnp.eye(order, dtype=jnp.float32))
    sel_rows = lax.broadcasted_iota(jnp.int32, (order, block_rows), 0)
    sel_cols = lax.broadcasted_iota(jnp.int32, (order, block_rows), 1) + train_index * block_rows
    selector = (sel_rows == sel_cols).astype(jnp.float32)
    halfway = lax.linalg.triangular_solve(factor, selector, left_side=True, lower=True)
    inverse_cols = lax.linalg.triangular_solve(
        factor, halfway, left_side=True, lower=True, transpose_a=True
    )
    return jnp.dot(
        lax.all_gather(cross_tile, "train", axis=1, tiled=True),
        inverse_cols,
        precision=HIGHEST,
        preferred_element_type=jnp.float32,
    )


def solution(mesh):
    sizes = mesh.shape["train"], mesh.shape["query"], mesh.shape["feat"]

    def on_device(train_pool, query_pool, train_pick, query_pick):
        order = train_pick.shape[0] * sizes[0]
        fits = (
            order == 128
            and order % (8 * sizes[0] * sizes[1] * sizes[2]) == 0
            and train_pool.shape[1] % (128 * sizes[0] * sizes[1]) == 0
        )
        if fits:
            return with_kernels(sizes, train_pool, query_pool, train_pick, query_pick)
        return with_arrays(train_pool, query_pool, train_pick, query_pick)

    return jax.shard_map(
        on_device,
        mesh=mesh,
        in_specs=(
            P(("groups", "train"), "feat"),
            P(("groups", "query"), "feat"),
            P(("groups", "train")),
            P(("groups", "query")),
        ),
        out_specs=P(("groups", "query"), "train"),
        check_vma=False,
    )
```

```python
import functools

import jax
import jax.numpy as jnp
from jax import lax
from jax.experimental import pallas as pl
from jax.experimental.pallas import tpu as pltpu
from jax.sharding import PartitionSpec as P

WIDTH = 8192
HIGHEST = lax.Precision.HIGHEST
NT = (((1,), (1,)), ((), ()))
CHUNKS = 4


def dot_nt(a, b):
    return lax.dot_general(a, b, NT, precision=HIGHEST, preferred_element_type=jnp.float32)


def parts(x):
    high = x.astype(jnp.bfloat16)
    rest = x - high.astype(jnp.float32)
    middle = rest.astype(jnp.bfloat16)
    low = (rest - middle.astype(jnp.float32)).astype(jnp.bfloat16)
    return high, middle, low


def invert(kernel_ref, inverse):
    order = kernel_ref.shape[0]
    lane = lax.broadcasted_iota(jnp.int32, (8, order), 1)
    sub = lax.broadcasted_iota(jnp.int32, (8, order), 0)
    tiles = []
    for i in range(order // 8):
        diagonal = lane == sub + 8 * i
        tiles.append(kernel_ref[8 * i : 8 * i + 8, :] * (1 / WIDTH) + jnp.where(diagonal, 0.5, 0.0))

    def columns(tile, k):
        return [jnp.broadcast_to(tile[:, k + j : k + j + 1], (8, order)) for j in range(4)]

    def row(tile, r):
        return jnp.broadcast_to(tile[r : r + 1, :], (8, order))

    for k in range(0, order, 4):
        home, r = k // 8, k % 8
        pivots = columns(tiles[home], k)
        a00, a01, a02, a03 = (row(pivots[j], r) for j in range(4))
        a11, a12, a13 = (row(pivots[j], r + 1) for j in range(1, 4))
        a22, a23 = (row(pivots[j], r + 2) for j in range(2, 4))
        a33 = row(pivots[3], r + 3)
        in_pivot = (lane >= k) & (lane < k + 4)
        r0, r1, r2, r3 = (
            jnp.where(in_pivot, jnp.where(lane == k + j, 1.0, 0.0), row(tiles[home], r + j))
            for j in range(4)
        )
        det = a00 * a11 - a01 * a01
        y00, y01 = a11 * a02 - a01 * a12, a11 * a03 - a01 * a13
        y10, y11 = a00 * a12 - a01 * a02, a00 * a13 - a01 * a03
        s00 = det * a22 - (a02 * y00 + a12 * y10)
        s01 = det * a23 - (a02 * y01 + a12 * y11)
        s11 = det * a33 - (a03 * y01 + a13 * y11)
        first = 1.0 / det
        second = det * (1.0 / (s00 * s11 - s01 * s01))
        d00, d01, d11 = a11 * first, -a01 * first, a00 * first
        x00, x01, x10, x11 = y00 * first, y01 * first, y10 * first, y11 * first
        e00, e01, e11 = s11 * second, -s01 * second, s00 * second
        v2 = r2 - (x00 * r0 + x10 * r1)
        v3 = r3 - (x01 * r0 + x11 * r1)
        w2 = e00 * v2 + e01 * v3
        w3 = e01 * v2 + e11 * v3
        w0 = (d00 * r0 + d01 * r1) - (x00 * w2 + x01 * w3)
        w1 = (d01 * r0 + d11 * r1) - (x10 * w2 + x11 * w3)
        following = min(k + 4, order - 1) // 8
        for i in sorted(range(order // 8), key=lambda i: i != following):
            c = pivots if i == home else columns(tiles[i], k)
            new = jnp.where(in_pivot, 0.0, tiles[i])
            new = new - ((c[0] * w0 + c[1] * w1) + (c[2] * w2 + c[3] * w3))
            if i == home:
                for j, w in enumerate((w0, w1, w2, w3)):
                    new = jnp.where(sub == r + j, w, new)
            tiles[i] = new
    for i in range(order // 8):
        inverse[8 * i : 8 * i + 8, :] = tiles[i]


def products(n_train, n_query, n_feat, train_pick_in, query_pick_in, train_pool, query_pool,
             scores_out, train_pick, query_pick,
             train_buf, query_buf, rows, blocks, part, terms, slab, full, inverse, mine, other, tile, crosses,
             local_sem, a2a_send, a2a_recv, rs_send, rs_recv, ag_send, ag_recv,
             pair_send, pair_recv, tile_send, tile_recv):
    g = lax.axis_index("groups")
    t = lax.axis_index("train")
    q = lax.axis_index("query")
    f = lax.axis_index("feat")
    n_pool, width = train_pool.shape
    block_rows = train_pick.shape[0]
    step = width // CHUNKS
    load_train = pltpu.make_async_copy(train_pool, train_buf, local_sem.at[CHUNKS])
    load_train.start()
    load_picks = [
        pltpu.make_async_copy(train_pick_in, train_pick, local_sem.at[CHUNKS + 1]),
        pltpu.make_async_copy(query_pick_in, query_pick, local_sem.at[CHUNKS + 2]),
    ]
    for load in load_picks:
        load.start()
    offsets = [
        (a, b, c) for a in range(n_train) for b in range(n_query) for c in range(n_feat)
    ][:0:-1]

    def peer(a, b, c):
        return lax.rem(t + a, n_train), lax.rem(q + b, n_query), lax.rem(f + c, n_feat)

    def device(where):
        return (g, where[0], where[1], where[2])

    def place(where):
        return (where[0] * n_query + where[1]) * n_feat + where[2]

    barrier = pltpu.get_barrier_semaphore()
    for off in offsets:
        pl.semaphore_signal(
            barrier, inc=1, device_id=device(peer(*off)), device_id_type=pl.DeviceIdType.MESH
        )

    loads = []
    for c in range(CHUNKS):
        cols = pl.ds(c * step, step)
        load = pltpu.make_async_copy(query_pool.at[:, cols], query_buf.at[:, cols], local_sem.at[c])
        load.start()
        loads.append(load)
    for load in load_picks:
        load.wait()
    load_train.wait()
    named = [jnp.clip(train_pick[r] - t * n_pool, 0, n_pool - 1) for r in range(block_rows)]
    share = width // (n_train * n_query)

    def share_of(a, b):
        where = peer(a, b, 0)
        return pl.ds(pl.multiple_of((where[0] * n_query + where[1]) * share, share), share)

    def select(cols):
        for r in range(block_rows):
            rows[r : r + 1, cols] = train_buf[pl.ds(named[r], 1), cols]

    select(share_of(1, 0))
    pl.semaphore_wait(barrier, len(offsets))

    def remote(src, dst, send, recv, where):
        copy = pltpu.make_async_remote_copy(
            src_ref=src, dst_ref=dst, send_sem=send, recv_sem=recv,
            device_id=device(where), device_id_type=pl.DeviceIdType.MESH,
        )
        copy.start()
        return copy

    a2a = []
    for a in range(1, n_train):
        cols = share_of(a, 0)
        if a > 1:
            select(cols)
        a2a.append(
            remote(rows.at[:, cols], blocks.at[t], a2a_send.at[a], a2a_recv.at[a], peer(a, 0, 0))
        )
    select(share_of(0, 0))
    blocks[t] = rows[:, share_of(0, 0)]
    for a in range(n_train):
        for b in range(1, n_query):
            select(share_of(a, b))

    total = None
    for c in range(CHUNKS):
        loads[c].wait()
        cols = slice(c * step, (c + 1) * step)
        x = parts(rows[:, cols])
        y = parts(query_buf[:, cols])
        term = 0.0
        for p in (2, 1, 0):
            stacked = lax.dot_general(
                jnp.concatenate(x[: 3 - p]), y[p], NT, preferred_element_type=jnp.float32
            )
            for i in reversed(range(3 - p)):
                term = term + stacked[i * block_rows : (i + 1) * block_rows]
        total = term if total is None else total + term
    n_query_pool = query_pool.shape[0]
    n_queries = query_pick.shape[1]
    chosen = (
        lax.broadcasted_iota(jnp.int32, (n_query_pool, n_queries), 0)
        == query_pick[...] - q * n_query_pool
    ).astype(jnp.float32)
    mine[...] = jnp.dot(total, chosen, precision=HIGHEST, preferred_element_type=jnp.float32)
    pair = remote(mine, other, pair_send, pair_recv, peer(0, 0, 1))

    for copy in a2a:
        copy.wait()
    gathered = blocks[...].reshape(n_train * block_rows, share)
    part[...] = dot_nt(gathered, gathered)
    slab_rows = slab.shape[0]

    def slab_of(where):
        return pl.ds(pl.multiple_of(place(where) * slab_rows, slab_rows), slab_rows)

    here = (t, q, f)
    rs = []
    for i, off in enumerate(offsets):
        where = peer(*off)
        rs.append(remote(part.at[slab_of(where)], terms.at[i], rs_send.at[i], rs_recv.at[i], where))

    pair.wait()
    tile[...] = mine[...] + other[...]
    crosses[t] = tile[...]
    tiles = []
    for a in range(1, n_train):
        tiles.append(remote(tile, crosses.at[t], tile_send.at[a], tile_recv.at[a], peer(a, 0, 0)))

    for copy in rs:
        copy.wait()
    summed = part[slab_of(here), :]
    for i in range(len(offsets)):
        summed = summed + terms[i]
    slab[...] = summed
    full[slab_of(here), :] = summed
    ag = []
    for i, off in enumerate(offsets):
        ag.append(remote(slab, full.at[slab_of(here)], ag_send.at[i], ag_recv.at[i], peer(*off)))
    for copy in ag:
        copy.wait()
    invert(full, inverse)
    for copy in tiles:
        copy.wait()
    start = pl.multiple_of(t * block_rows, block_rows)
    scores_out[...] = jnp.dot(
        inverse[pl.ds(start, block_rows), :],
        crosses[...].reshape(n_train * block_rows, n_queries),
        precision=HIGHEST,
        preferred_element_type=jnp.float32,
    )


def with_kernels(sizes, train_pool, query_pool, train_pick, query_pick):
    n_train, n_query, n_feat = sizes
    n_peers = n_train * n_query * n_feat
    block_rows = train_pick.shape[0]
    order = block_rows * n_train
    n_queries = query_pick.shape[0]
    width = train_pool.shape[1]
    share = width // (n_train * n_query)
    slab_rows = order // n_peers
    vmem = pl.BlockSpec(memory_space=pltpu.VMEM)
    hbm = pl.BlockSpec(memory_space=pltpu.HBM)
    f32 = jnp.float32
    dma = pltpu.SemaphoreType.DMA
    scores = pl.pallas_call(
        functools.partial(products, n_train, n_query, n_feat),
        out_shape=jax.ShapeDtypeStruct((block_rows, n_queries), f32),
        in_specs=[hbm] * 4,
        out_specs=vmem,
        scratch_shapes=[
            pltpu.SMEM((block_rows,), jnp.int32),
            pltpu.VMEM((1, n_queries), jnp.int32),
            pltpu.VMEM(train_pool.shape, f32),
            pltpu.VMEM(query_pool.shape, f32),
            pltpu.VMEM((block_rows, width), f32),
            pltpu.VMEM((n_train, block_rows, share), f32),
            pltpu.VMEM((order, order), f32),
            pltpu.VMEM((n_peers - 1, slab_rows, order), f32),
            pltpu.VMEM((slab_rows, order), f32),
            pltpu.VMEM((order, order), f32),
            pltpu.VMEM((order, order), f32),
            pltpu.VMEM((block_rows, n_queries), f32),
            pltpu.VMEM((block_rows, n_queries), f32),
            pltpu.VMEM((block_rows, n_queries), f32),
            pltpu.VMEM((n_train, block_rows, n_queries), f32),
            dma((CHUNKS + 3,)),
            dma((n_train,)), dma((n_train,)),
            dma((n_peers - 1,)), dma((n_peers - 1,)),
            dma((n_peers - 1,)), dma((n_peers - 1,)),
            dma, dma,
            dma((n_train,)), dma((n_train,)),
        ],
        compiler_params=pltpu.CompilerParams(
            collective_id=0, has_side_effects=True, vmem_limit_bytes=64 * 1024 * 1024
        ),
        name="products",
    )(train_pick, query_pick.reshape(1, n_queries), train_pool, query_pool)
    return scores.T * (1 / WIDTH)


def with_arrays(train_pool, query_pool, train_pick, query_pick):
    block_rows = train_pick.shape[0]
    train_index = lax.axis_index("train")
    query_index = lax.axis_index("query")
    train_rows = jnp.take(train_pool, train_pick - train_index * train_pool.shape[0], axis=0)
    query_rows = jnp.take(query_pool, query_pick - query_index * query_pool.shape[0], axis=0)
    cross_tile = dot_nt(query_rows, train_rows)
    kernel_part = dot_nt(train_rows, lax.all_gather(train_rows, "train", axis=0, tiled=True))
    cross_tile, kernel_part = lax.psum((cross_tile, kernel_part), "feat")
    kernel = lax.all_gather(kernel_part, "train", axis=0, tiled=True)
    order = kernel.shape[0]
    factor = jnp.linalg.cholesky(kernel + 0.5 * WIDTH * jnp.eye(order, dtype=jnp.float32))
    sel_rows = lax.broadcasted_iota(jnp.int32, (order, block_rows), 0)
    sel_cols = lax.broadcasted_iota(jnp.int32, (order, block_rows), 1) + train_index * block_rows
    selector = (sel_rows == sel_cols).astype(jnp.float32)
    halfway = lax.linalg.triangular_solve(factor, selector, left_side=True, lower=True)
    inverse_cols = lax.linalg.triangular_solve(
        factor, halfway, left_side=True, lower=True, transpose_a=True
    )
    return jnp.dot(
        lax.all_gather(cross_tile, "train", axis=1, tiled=True),
        inverse_cols,
        precision=HIGHEST,
        preferred_element_type=jnp.float32,
    )


def solution(mesh):
    sizes = mesh.shape["train"], mesh.shape["query"], mesh.shape["feat"]

    def on_device(train_pool, query_pool, train_pick, query_pick):
        order = train_pick.shape[0] * sizes[0]
        fits = (
            order == 128
            and order % (8 * sizes[0] * sizes[1] * sizes[2]) == 0
            and train_pool.shape[1] % (128 * sizes[0] * sizes[1]) == 0
        )
        if fits:
            return with_kernels(sizes, train_pool, query_pool, train_pick, query_pick)
        return with_arrays(train_pool, query_pool, train_pick, query_pick)

    return jax.shard_map(
        on_device,
        mesh=mesh,
        in_specs=(
            P(("groups", "train"), "feat"),
            P(("groups", "query"), "feat"),
            P(("groups", "train")),
            P(("groups", "query")),
        ),
        out_specs=P(("groups", "query"), "train"),
        check_vma=False,
    )
```

```python
import functools

import jax
import jax.numpy as jnp
from jax import lax
from jax.experimental import pallas as pl
from jax.experimental.pallas import tpu as pltpu
from jax.sharding import PartitionSpec as P

WIDTH = 8192
HIGHEST = lax.Precision.HIGHEST
NT = (((1,), (1,)), ((), ()))
CHUNKS = 4


def dot_nt(a, b):
    return lax.dot_general(a, b, NT, precision=HIGHEST, preferred_element_type=jnp.float32)


def parts(x):
    high = x.astype(jnp.bfloat16)
    rest = x - high.astype(jnp.float32)
    middle = rest.astype(jnp.bfloat16)
    low = (rest - middle.astype(jnp.float32)).astype(jnp.bfloat16)
    return high, middle, low


def inverse_2x2(a, b, d):
    scale = 1.0 / (a * d - b * b)
    return d * scale, -b * scale, a * scale


def invert(kernel_ref, inverse):
    order = kernel_ref.shape[0]
    lane = lax.broadcasted_iota(jnp.int32, (8, order), 1)
    sub = lax.broadcasted_iota(jnp.int32, (8, order), 0)
    tiles = []
    for i in range(order // 8):
        diagonal = lane == sub + 8 * i
        tiles.append(kernel_ref[8 * i : 8 * i + 8, :] + jnp.where(diagonal, 0.5 * WIDTH, 0.0))

    def columns(tile, k):
        return [jnp.broadcast_to(tile[:, k + j : k + j + 1], (8, order)) for j in range(4)]

    def row(tile, r):
        return jnp.broadcast_to(tile[r : r + 1, :], (8, order))

    for k in range(0, order, 4):
        home, r = k // 8, k % 8
        pivots = columns(tiles[home], k)
        a00, a01, a02, a03 = (row(pivots[j], r) for j in range(4))
        a11, a12, a13 = (row(pivots[j], r + 1) for j in range(1, 4))
        a22, a23 = (row(pivots[j], r + 2) for j in range(2, 4))
        a33 = row(pivots[3], r + 3)
        in_pivot = (lane >= k) & (lane < k + 4)
        r0, r1, r2, r3 = (
            jnp.where(in_pivot, jnp.where(lane == k + j, 1.0, 0.0), row(tiles[home], r + j))
            for j in range(4)
        )
        d00, d01, d11 = inverse_2x2(a00, a01, a11)
        x00, x01 = d00 * a02 + d01 * a12, d00 * a03 + d01 * a13
        x10, x11 = d01 * a02 + d11 * a12, d01 * a03 + d11 * a13
        e00, e01, e11 = inverse_2x2(
            a22 - (a02 * x00 + a12 * x10),
            a23 - (a02 * x01 + a12 * x11),
            a33 - (a03 * x01 + a13 * x11),
        )
        v2 = r2 - (x00 * r0 + x10 * r1)
        v3 = r3 - (x01 * r0 + x11 * r1)
        w2 = e00 * v2 + e01 * v3
        w3 = e01 * v2 + e11 * v3
        w0 = (d00 * r0 + d01 * r1) - (x00 * w2 + x01 * w3)
        w1 = (d01 * r0 + d11 * r1) - (x10 * w2 + x11 * w3)
        following = min(k + 4, order - 1) // 8
        for i in sorted(range(order // 8), key=lambda i: i != following):
            c = pivots if i == home else columns(tiles[i], k)
            new = jnp.where(in_pivot, 0.0, tiles[i])
            new = new - ((c[0] * w0 + c[1] * w1) + (c[2] * w2 + c[3] * w3))
            if i == home:
                for j, w in enumerate((w0, w1, w2, w3)):
                    new = jnp.where(sub == r + j, w, new)
            tiles[i] = new
    for i in range(order // 8):
        inverse[8 * i : 8 * i + 8, :] = tiles[i]


def products(n_train, n_query, n_feat, train_pick_in, query_pick_in, train_pool, query_pool,
             scores_out, train_pick, query_pick,
             train_buf, query_buf, rows, blocks, part, terms, slab, full, inverse, mine, other, tile, crosses,
             local_sem, a2a_send, a2a_recv, rs_send, rs_recv, ag_send, ag_recv,
             pair_send, pair_recv, tile_send, tile_recv):
    g = lax.axis_index("groups")
    t = lax.axis_index("train")
    q = lax.axis_index("query")
    f = lax.axis_index("feat")
    n_pool, width = train_pool.shape
    block_rows = train_pick.shape[0]
    step = width // CHUNKS
    load_train = pltpu.make_async_copy(train_pool, train_buf, local_sem.at[CHUNKS])
    load_train.start()
    load_picks = [
        pltpu.make_async_copy(train_pick_in, train_pick, local_sem.at[CHUNKS + 1]),
        pltpu.make_async_copy(query_pick_in, query_pick, local_sem.at[CHUNKS + 2]),
    ]
    for load in load_picks:
        load.start()
    offsets = [
        (a, b, c) for a in range(n_train) for b in range(n_query) for c in range(n_feat)
    ][:0:-1]

    def peer(a, b, c):
        return lax.rem(t + a, n_train), lax.rem(q + b, n_query), lax.rem(f + c, n_feat)

    def device(where):
        return (g, where[0], where[1], where[2])

    def place(where):
        return (where[0] * n_query + where[1]) * n_feat + where[2]

    barrier = pltpu.get_barrier_semaphore()
    for off in offsets:
        pl.semaphore_signal(
            barrier, inc=1, device_id=device(peer(*off)), device_id_type=pl.DeviceIdType.MESH
        )

    loads = []
    for c in range(CHUNKS):
        cols = pl.ds(c * step, step)
        load = pltpu.make_async_copy(query_pool.at[:, cols], query_buf.at[:, cols], local_sem.at[c])
        load.start()
        loads.append(load)
    for load in load_picks:
        load.wait()
    load_train.wait()
    named = [jnp.clip(train_pick[r] - t * n_pool, 0, n_pool - 1) for r in range(block_rows)]
    share = width // (n_train * n_query)

    def share_of(a, b):
        where = peer(a, b, 0)
        return pl.ds(pl.multiple_of((where[0] * n_query + where[1]) * share, share), share)

    def select(cols):
        for r in range(block_rows):
            rows[r : r + 1, cols] = train_buf[pl.ds(named[r], 1), cols]

    select(share_of(1, 0))
    pl.semaphore_wait(barrier, len(offsets))

    def remote(src, dst, send, recv, where):
        copy = pltpu.make_async_remote_copy(
            src_ref=src, dst_ref=dst, send_sem=send, recv_sem=recv,
            device_id=device(where), device_id_type=pl.DeviceIdType.MESH,
        )
        copy.start()
        return copy

    a2a = []
    for a in range(1, n_train):
        cols = share_of(a, 0)
        if a > 1:
            select(cols)
        a2a.append(
            remote(rows.at[:, cols], blocks.at[t], a2a_send.at[a], a2a_recv.at[a], peer(a, 0, 0))
        )
    select(share_of(0, 0))
    blocks[t] = rows[:, share_of(0, 0)]
    for a in range(n_train):
        for b in range(1, n_query):
            select(share_of(a, b))

    total = None
    for c in range(CHUNKS):
        loads[c].wait()
        cols = slice(c * step, (c + 1) * step)
        x = parts(rows[:, cols])
        y = parts(query_buf[:, cols])
        term = 0.0
        for p in (2, 1, 0):
            stacked = lax.dot_general(
                jnp.concatenate(x[: 3 - p]), y[p], NT, preferred_element_type=jnp.float32
            )
            for i in reversed(range(3 - p)):
                term = term + stacked[i * block_rows : (i + 1) * block_rows]
        total = term if total is None else total + term
    n_query_pool = query_pool.shape[0]
    n_queries = query_pick.shape[1]
    chosen = (
        lax.broadcasted_iota(jnp.int32, (n_query_pool, n_queries), 0)
        == query_pick[...] - q * n_query_pool
    ).astype(jnp.float32)
    mine[...] = jnp.dot(total, chosen, precision=HIGHEST, preferred_element_type=jnp.float32)
    pair = remote(mine, other, pair_send, pair_recv, peer(0, 0, 1))

    for copy in a2a:
        copy.wait_recv()
    gathered = blocks[...].reshape(n_train * block_rows, share)
    part[...] = dot_nt(gathered, gathered)
    slab_rows = slab.shape[0]

    def slab_of(where):
        return pl.ds(pl.multiple_of(place(where) * slab_rows, slab_rows), slab_rows)

    here = (t, q, f)
    rs = []
    for i, off in enumerate(offsets):
        where = peer(*off)
        rs.append(remote(part.at[slab_of(where)], terms.at[i], rs_send.at[i], rs_recv.at[i], where))

    pair.wait_recv()
    tile[...] = mine[...] + other[...]
    crosses[t] = tile[...]
    tiles = []
    for a in range(1, n_train):
        tiles.append(remote(tile, crosses.at[t], tile_send.at[a], tile_recv.at[a], peer(a, 0, 0)))

    for copy in rs:
        copy.wait_recv()
    summed = part[slab_of(here), :]
    for i in range(len(offsets)):
        summed = summed + terms[i]
    slab[...] = summed
    full[slab_of(here), :] = summed
    ag = []
    for i, off in enumerate(offsets):
        ag.append(remote(slab, full.at[slab_of(here)], ag_send.at[i], ag_recv.at[i], peer(*off)))
    for copy in ag:
        copy.wait_recv()
    invert(full, inverse)
    for copy in tiles:
        copy.wait_recv()
    start = pl.multiple_of(t * block_rows, block_rows)
    scores_out[...] = jnp.dot(
        inverse[pl.ds(start, block_rows), :],
        crosses[...].reshape(n_train * block_rows, n_queries),
        precision=HIGHEST,
        preferred_element_type=jnp.float32,
    )
    for copy in a2a + [pair] + rs + tiles + ag:
        copy.wait_send()


def with_kernels(sizes, train_pool, query_pool, train_pick, query_pick):
    n_train, n_query, n_feat = sizes
    n_peers = n_train * n_query * n_feat
    block_rows = train_pick.shape[0]
    order = block_rows * n_train
    n_queries = query_pick.shape[0]
    width = train_pool.shape[1]
    share = width // (n_train * n_query)
    slab_rows = order // n_peers
    vmem = pl.BlockSpec(memory_space=pltpu.VMEM)
    hbm = pl.BlockSpec(memory_space=pltpu.HBM)
    f32 = jnp.float32
    dma = pltpu.SemaphoreType.DMA
    scores = pl.pallas_call(
        functools.partial(products, n_train, n_query, n_feat),
        out_shape=jax.ShapeDtypeStruct((block_rows, n_queries), f32),
        in_specs=[hbm] * 4,
        out_specs=vmem,
        scratch_shapes=[
            pltpu.SMEM((block_rows,), jnp.int32),
            pltpu.VMEM((1, n_queries), jnp.int32),
            pltpu.VMEM(train_pool.shape, f32),
            pltpu.VMEM(query_pool.shape, f32),
            pltpu.VMEM((block_rows, width), f32),
            pltpu.VMEM((n_train, block_rows, share), f32),
            pltpu.VMEM((order, order), f32),
            pltpu.VMEM((n_peers - 1, slab_rows, order), f32),
            pltpu.VMEM((slab_rows, order), f32),
            pltpu.VMEM((order, order), f32),
            pltpu.VMEM((order, order), f32),
            pltpu.VMEM((block_rows, n_queries), f32),
            pltpu.VMEM((block_rows, n_queries), f32),
            pltpu.VMEM((block_rows, n_queries), f32),
            pltpu.VMEM((n_train, block_rows, n_queries), f32),
            dma((CHUNKS + 3,)),
            dma((n_train,)), dma((n_train,)),
            dma((n_peers - 1,)), dma((n_peers - 1,)),
            dma((n_peers - 1,)), dma((n_peers - 1,)),
            dma, dma,
            dma((n_train,)), dma((n_train,)),
        ],
        compiler_params=pltpu.CompilerParams(
            collective_id=0, has_side_effects=True, vmem_limit_bytes=64 * 1024 * 1024
        ),
        name="products",
    )(train_pick, query_pick.reshape(1, n_queries), train_pool, query_pool)
    return scores.T


def with_arrays(train_pool, query_pool, train_pick, query_pick):
    block_rows = train_pick.shape[0]
    train_index = lax.axis_index("train")
    query_index = lax.axis_index("query")
    train_rows = jnp.take(train_pool, train_pick - train_index * train_pool.shape[0], axis=0)
    query_rows = jnp.take(query_pool, query_pick - query_index * query_pool.shape[0], axis=0)
    cross_tile = dot_nt(query_rows, train_rows)
    kernel_part = dot_nt(train_rows, lax.all_gather(train_rows, "train", axis=0, tiled=True))
    cross_tile, kernel_part = lax.psum((cross_tile, kernel_part), "feat")
    kernel = lax.all_gather(kernel_part, "train", axis=0, tiled=True)
    order = kernel.shape[0]
    factor = jnp.linalg.cholesky(kernel + 0.5 * WIDTH * jnp.eye(order, dtype=jnp.float32))
    sel_rows = lax.broadcasted_iota(jnp.int32, (order, block_rows), 0)
    sel_cols = lax.broadcasted_iota(jnp.int32, (order, block_rows), 1) + train_index * block_rows
    selector = (sel_rows == sel_cols).astype(jnp.float32)
    halfway = lax.linalg.triangular_solve(factor, selector, left_side=True, lower=True)
    inverse_cols = lax.linalg.triangular_solve(
        factor, halfway, left_side=True, lower=True, transpose_a=True
    )
    return jnp.dot(
        lax.all_gather(cross_tile, "train", axis=1, tiled=True),
        inverse_cols,
        precision=HIGHEST,
        preferred_element_type=jnp.float32,
    )


def solution(mesh):
    sizes = mesh.shape["train"], mesh.shape["query"], mesh.shape["feat"]

    def on_device(train_pool, query_pool, train_pick, query_pick):
        order = train_pick.shape[0] * sizes[0]
        fits = (
            order == 128
            and order % (8 * sizes[0] * sizes[1] * sizes[2]) == 0
            and train_pool.shape[1] % (128 * sizes[0] * sizes[1]) == 0
        )
        if fits:
            return with_kernels(sizes, train_pool, query_pool, train_pick, query_pick)
        return with_arrays(train_pool, query_pool, train_pick, query_pick)

    return jax.shard_map(
        on_device,
        mesh=mesh,
        in_specs=(
            P(("groups", "train"), "feat"),
            P(("groups", "query"), "feat"),
            P(("groups", "train")),
            P(("groups", "query")),
        ),
        out_specs=P(("groups", "query"), "train"),
        check_vma=False,
    )
```
